256 devices in a mesh: row: 16 (over y, z_hi), col: 16 (over x, z_lo, core).
Axes of the slice: x: 4, y: 4, z: 8 (z_hi: 4, z_lo: 2; z = z_hi * 2 + z_lo), core: 2. Of those that a mesh axis runs over, the one named last changes fastest.
Arguments:
- queries: bfloat16 [192, 768, 128], P('row', 'col'), may hold values from -6 to 6
- keys_values: bfloat16 [192, 768, 256], P('row', 'col'), may hold values from -6 to 6
- out_grad: bfloat16 [192, 768, 128], P('row', 'col'), may hold values from -48 to 48
- pair_bias: bfloat16 [4, 768, 768], P(None, 'row', 'col'), may hold values from -6 to 6
- log_norm: float32 [4, 192, 768], P(None, 'row', 'col'), may hold values from 7.2 to 8.6
- delta_rows: float32 [4, 192, 768], P(None, 'row', 'col'), may hold values from -96 to 96
- token_valid: int32 [768], replicated, may hold values from 0 to 1, as said below
Outputs:
- query_grad: bfloat16 [192, 768, 128], P('row', 'col')
- kv_grad: bfloat16 [768, 192, 256], P('col', 'row')
- bias_grad: float32 [4, 768, 768], P(None, 'row', 'col')
The draws below stay inside these ranges and needn't reach their ends.
Inputs may be any that keep to these rules, and one draw needn't show every extreme that they name: `token_valid`: 1 for the first tokens and 0 for a padded tail; at least 384 ones and at least one 0.
All inputs are finite; a program needn't handle non-finite values.
Results may differ from the reference program's by a relative error of at most 0.025.
Values may be sent and summed in bfloat16 or wider, within the bound.
No kernel may reach another device: no remote copies, remote signals or barrier semaphores. Data moves between devices by JAX's collectives and lax.ppermute only.
A program may use at most 64 MiB of HBM per device.

```python
import jax
import jax.numpy as jnp
from jax import lax

HEADS = 4
WIDTH = 128
TOKENS = 768
QUERY_ROWS = 192
N_COL = 16


def draw_token_valid(key, part):
    key = jax.random.fold_in(key, 7)
    valid_len = jax.random.randint(key, (), TOKENS // 2, TOKENS)
    return (jnp.arange(TOKENS) < valid_len).astype(jnp.int32)


def steps_of(stream_key, shape, pieces, smallest, largest):
    loudness = 1.0
    for axis_at, blocks in pieces:
        steps = jax.random.uniform(jax.random.fold_in(jax.random.fold_in(stream_key, 6), axis_at), (blocks,), jnp.float32, smallest / len(pieces), largest / len(pieces))
        loudness = loudness * jnp.repeat(jnp.exp(steps), shape[axis_at] // blocks).reshape((-1,) + (1,) * (len(shape) - 1 - axis_at))
    return loudness


def noise(own_key, dims, width, most, cuts=(), dtype=jnp.bfloat16):
    drawn = jax.random.normal(own_key, dims, jnp.float32) * width
    if len(cuts) > 0:
        drawn = steps_of(own_key, dims, cuts, -0.22, 0.18) * drawn
    return jnp.clip(drawn, min=-most, max=most).astype(dtype)


def setup_inputs(seed: int = 0) -> dict:
    splits = jax.random.split(jax.random.key(seed), 8)
    queries = noise(splits[0], (QUERY_ROWS, TOKENS, WIDTH), 1.0, 6.0, ((0, 16), (1, 16)))
    keys_values = noise(splits[1], (QUERY_ROWS, TOKENS, 2 * WIDTH), 1.0, 6.0, ((0, 16), (1, 16)))
    out_grad = noise(splits[2], (QUERY_ROWS, TOKENS, WIDTH), 8.0, 48.0, ((0, 16), (1, 16)))
    pair_bias = noise(splits[3], (HEADS, TOKENS, TOKENS), 1.0, 6.0, ((1, 16), (2, 16)))
    log_norm = jnp.clip(7.2 + 1.4000006 * jax.random.uniform(splits[4], (HEADS, QUERY_ROWS, TOKENS), jnp.float32) ** steps_of(splits[4], (HEADS, QUERY_ROWS, TOKENS), ((1, 16), (2, 16)), -0.2, 0.2), 7.2, 8.6)
    delta_rows = noise(splits[5], (HEADS, QUERY_ROWS, TOKENS), 16.0, 96.0, ((1, 16), (2, 16)), jnp.float32)
    token_valid = draw_token_valid(jax.random.fold_in(splits[7], 71), 0)
    return dict(queries=queries, keys_values=keys_values, out_grad=out_grad, pair_bias=pair_bias, log_norm=log_norm, delta_rows=delta_rows, token_valid=token_valid)


def reference(queries, keys_values, out_grad, pair_bias, log_norm, delta_rows, token_valid):
    row_total, key_count, channels = queries.shape
    head_count = pair_bias.shape[0]
    head_size = channels // head_count
    inv_root = head_size ** -0.5
    key_bias = jnp.where(token_valid == 1, 0.0, -10000.0).astype(jnp.float32)
    full_bias = pair_bias.astype(jnp.float32) + key_bias[None, None, :]
    norm_rows = jnp.transpose(log_norm, (1, 0, 2))
    delta_now = jnp.transpose(delta_rows, (1, 0, 2))
    block_len = key_count // N_COL

    def one_row(bias_total, slices):
        query_row, kv_row, grad_row, norm_row, delta_row = slices
        query_heads = query_row.astype(jnp.float32).reshape(key_count, head_count, head_size)
        key_heads = kv_row[:, :channels].astype(jnp.float32).reshape(key_count, head_count, head_size)
        value_heads = kv_row[:, channels:].astype(jnp.float32).reshape(key_count, head_count, head_size)
        grad_heads = grad_row.astype(jnp.float32).reshape(key_count, head_count, head_size)
        scores = jnp.einsum("jhd,khd->hjk", query_heads, key_heads) * inv_root + full_bias
        probs = jnp.exp(scores - norm_row[:, :, None])
        prob_grad = jnp.einsum("jhd,khd->hjk", grad_heads, value_heads)
        score_grad = probs * (prob_grad - delta_row[:, :, None])
        score_low = lax.optimization_barrier(score_grad.astype(jnp.bfloat16)).astype(jnp.float32)
        probs_low = lax.optimization_barrier(probs.astype(jnp.bfloat16)).astype(jnp.float32)
        query_out = (jnp.einsum("hjk,khd->jhd", score_low, key_heads) * inv_root).reshape(key_count, channels)
        score_blocks = score_low.reshape(head_count, N_COL, block_len, key_count)
        prob_blocks = probs_low.reshape(head_count, N_COL, block_len, key_count)
        query_blocks = query_heads.reshape(N_COL, block_len, head_count, head_size)
        grad_blocks = grad_heads.reshape(N_COL, block_len, head_count, head_size)
        key_part = jnp.einsum("hbjk,bjhd->bkhd", score_blocks, query_blocks) * inv_root
        value_part = jnp.einsum("hbjk,bjhd->bkhd", prob_blocks, grad_blocks)
        block_parts = jnp.concatenate([key_part.reshape(N_COL, key_count, channels), value_part.reshape(N_COL, key_count, channels)], axis=-1)
        block_parts = lax.optimization_barrier(block_parts.astype(jnp.bfloat16)).astype(jnp.float32)
        kv_out = jnp.sum(block_parts, axis=0).astype(jnp.bfloat16)
        return bias_total + score_grad, (query_out.astype(jnp.bfloat16), kv_out)

    start_bias = jnp.zeros((head_count, key_count, key_count), jnp.float32)
    bias_grad, (query_grad, kv_rows) = lax.scan(one_row, start_bias, (queries, keys_values, out_grad, norm_rows, delta_now))
    return query_grad, jnp.transpose(kv_rows, (1, 0, 2)), bias_grad
```

```python
import functools
import math

import jax
import jax.numpy as jnp
from jax import lax
from jax.experimental import pallas as pl
from jax.experimental.pallas import tpu as pltpu
from jax.sharding import Mesh, PartitionSpec as P

BF = jnp.bfloat16
F32 = jnp.float32
LANES = 128


def call(body, name, out_shape, scratch=(), smem=(), n_in=1, limit=48 << 20):
    in_specs = [
        pl.BlockSpec(memory_space=pltpu.SMEM if i in smem else pltpu.VMEM) for i in range(n_in)
    ]
    out_specs = jax.tree.map(lambda _: pl.BlockSpec(memory_space=pltpu.VMEM), out_shape)
    return pl.pallas_call(
        body,
        name=name,
        out_shape=out_shape,
        in_specs=in_specs,
        out_specs=out_specs,
        scratch_shapes=list(scratch),
        compiler_params=pltpu.CompilerParams(vmem_limit_bytes=limit),
    )


def pack_kernel(root, q_ref, kv_ref, g_ref, bias_ref, norm_ref, delta_ref, mask_ref, out_ref, rows):
    heads, cols, _ = bias_ref.shape
    n_i, _, width = q_ref.shape
    size = width // heads
    pairs = n_i // 2
    for h in range(heads):
        lo, hi = h * size, (h + 1) * size
        for p in range(pairs):
            out_ref[h, p] = jnp.concatenate(
                [
                    q_ref[2 * p, :, lo:hi],
                    g_ref[2 * p, :, lo:hi],
                    q_ref[2 * p + 1, :, lo:hi],
                    g_ref[2 * p + 1, :, lo:hi],
                ],
                axis=-1,
            )
            out_ref[h, pairs + p] = jnp.concatenate(
                [
                    kv_ref[2 * p, :, lo:hi],
                    kv_ref[2 * p, :, width + lo : width + hi],
                    kv_ref[2 * p + 1, :, lo:hi],
                    kv_ref[2 * p + 1, :, width + lo : width + hi],
                ],
                axis=-1,
            )
        rows[...] = jnp.zeros_like(rows)
        norm = norm_ref[h] * root
        high = norm.astype(BF).astype(F32)
        rows[0:n_i, 0:cols] = high
        rows[16 : 16 + n_i, 0:cols] = norm - high
        delta = delta_ref[h]
        high = delta.astype(BF).astype(F32)
        rows[32 : 32 + n_i, 0:cols] = high
        rows[48 : 48 + n_i, 0:cols] = delta - high
        turned = jnp.transpose(rows[...])[0:cols]
        tile = bias_ref[h].astype(F32) + mask_ref[...]
        out_ref[h, 2 * pairs] = jnp.concatenate(
            [turned[:, 0:64], tile, jnp.zeros((cols, 64 - cols), F32)], axis=-1
        ).astype(BF)


def unpack_kernel(got_ref, a_ref, bias_ref):
    parts, blocks, cols, _ = got_ref.shape
    pairs = blocks // 2
    for p in range(pairs):
        a_ref[p] = got_ref[:, p].reshape(parts * cols, LANES)
    a_ref[pairs] = got_ref[:, blocks - 1].reshape(parts * cols, LANES)
    pieces = [got_ref[x, blocks - 1, :, 64 : 64 + cols].astype(F32) for x in range(parts)]
    pieces.append(jnp.zeros((cols, bias_ref.shape[2] - parts * cols), F32))
    band = jnp.concatenate(pieces, axis=-1).astype(BF)
    for r in range(bias_ref.shape[0]):
        bias_ref[r] = band


def main_kernel(
    inv_root,
    place_ref,
    got_ref,
    a0_ref,
    a1_ref,
    a2_ref,
    a3_ref,
    bias_ref,
    dq_ref,
    dkv_ref,
    dbias_ref,
    rows,
    bias_t,
    acc,
    dq_t,
):
    parts, blocks, cols, _ = got_ref.shape
    pairs = blocks // 2
    keys = parts * cols
    total = 4 * keys
    size = 32
    log2e = math.log2(math.e)
    zl, core = place_ref[0], place_ref[1]

    def row_of(b, x):
        return x * 4 + jnp.bitwise_xor(zl, b // 2) * 2 + jnp.bitwise_xor(core, b % 2)

    for b in range(4):
        for x in range(parts):
            at = b * keys + x * cols
            rows[at : at + cols] = bias_ref[row_of(b, x)].astype(F32)
    for t in range(0, total, LANES):
        bias_t[:, t : t + LANES] = (
            jnp.transpose(rows[t : t + LANES])[0:keys] * log2e
        )
    acc[...] = jnp.zeros_like(acc)
    lane = lax.broadcasted_iota(jnp.int32, (keys, LANES), 1)
    quarter = lax.broadcasted_iota(jnp.int32, (total, LANES), 1) // size
    a_refs = (a0_ref, a1_ref, a2_ref, a3_ref)
    extra = jnp.concatenate([a[pairs] for a in a_refs], axis=0)
    scale_row = jnp.where((lane // size) % 2 == 0, inv_root, 1.0)
    chunk = 256
    for p in range(pairs):
        qp = jnp.concatenate([a[p] for a in a_refs], axis=0)
        qx = jnp.concatenate([qp, extra], axis=1)
        kp = got_ref[:, pairs + p].reshape(keys, LANES)
        kt = jnp.transpose(kp.astype(F32)).astype(BF)
        zero = jnp.zeros_like(kp)
        left = []
        for s in range(4):
            i = 2 * p + s // 2
            base = 32 * (s % 2)
            ones = jnp.where((lane == base + i) | (lane == base + 16 + i), -1.0, 0.0).astype(BF)
            left.append(
                jnp.concatenate([jnp.where(lane // size == s, kp, zero), ones], axis=1)
            )
        qm = [jnp.where(quarter == s, qp, jnp.zeros_like(qp)) for s in range(4)]
        out = jnp.zeros((keys, LANES), F32)
        for t in range(0, total, chunk):
            here = qx[t : t + chunk]
            for e in range(2):
                scores = lax.dot_general(
                    left[2 * e], here, (((1,), (1,)), ((), ())), preferred_element_type=F32
                )
                grads = lax.dot_general(
                    left[2 * e + 1], here, (((1,), (1,)), ((), ())), preferred_element_type=F32
                )
                probs = jnp.exp2(scores * (inv_root * log2e) + bias_t[:, t : t + chunk])
                ds = probs * grads
                acc[:, t : t + chunk] += ds
                ds_low = ds.astype(BF)
                out += jnp.dot(ds_low, qm[2 * e][t : t + chunk], preferred_element_type=F32)
                out += jnp.dot(
                    probs.astype(BF), qm[2 * e + 1][t : t + chunk], preferred_element_type=F32
                )
                i = 2 * p + e
                dq_t[i * size : (i + 1) * size, t : t + chunk] = jnp.dot(
                    kt[2 * e * size : (2 * e + 1) * size], ds_low, preferred_element_type=F32
                )
        dkv_ref[p] = (out * scale_row).astype(BF)
    for quad in range(2 * pairs // 4):
        turned = jnp.transpose(dq_t[quad * LANES : (quad + 1) * LANES]) * inv_root
        for b in range(4):
            dq_ref[b, quad] = turned[b * keys : (b + 1) * keys].astype(BF)
    for t in range(0, total, LANES):
        rows[t : t + LANES, 0:keys] = jnp.transpose(acc[:, t : t + LANES])
    for b in range(4):
        for x in range(parts):
            at = b * keys + x * cols
            dbias_ref[row_of(b, x)] = rows[at : at + cols].astype(BF)


def merge_kernel(dq_ref, r1_ref, r2_ref, r3_ref, dkv_ref, db_ref, out_ref):
    parts, _, cols, _ = out_ref.shape
    quads = dq_ref.shape[0]
    pairs = dkv_ref.shape[0]
    total = (
        dq_ref[...].astype(F32)
        + r1_ref[...].astype(F32)
        + r2_ref[...].astype(F32)
        + r3_ref[...].astype(F32)
    ).astype(BF)
    bias = db_ref[0].astype(F32)
    for r in range(1, db_ref.shape[0]):
        bias = bias + db_ref[r].astype(F32)
    for x in range(parts):
        lo, hi = x * cols, (x + 1) * cols
        for quad in range(quads):
            out_ref[x, quad] = total[quad, lo:hi]
        for p in range(pairs):
            out_ref[x, quads + p] = dkv_ref[p, lo:hi]
        out_ref[x, quads + pairs] = jnp.concatenate(
            [bias[:, lo:hi], jnp.zeros((cols, LANES - cols), F32)], axis=-1
        ).astype(BF)


def final_kernel(got_ref, dq_ref, dkv_ref, db_ref, turn):
    heads, blocks, cols, _ = got_ref.shape
    size = 32
    n_i = dq_ref.shape[0]
    quads = n_i // 4
    pairs = n_i // 2
    for i in range(n_i):
        at = (i % 4) * size
        dq_ref[i] = jnp.concatenate(
            [got_ref[h, i // 4, :, at : at + size] for h in range(heads)], axis=-1
        )
        at = (i % 2) * 2 * size
        row = jnp.concatenate(
            [got_ref[h, quads + i // 2, :, at : at + size] for h in range(heads)]
            + [got_ref[h, quads + i // 2, :, at + size : at + 2 * size] for h in range(heads)],
            axis=-1,
        )
        turn[:, i, :] = row.astype(F32)
    dkv_ref[...] = turn[:, 0:n_i, :].astype(BF)
    for h in range(heads):
        db_ref[h] = got_ref[h, blocks - 1, :, 0:cols].astype(F32)


def on_device(queries, keys_values, out_grad, pair_bias, log_norm, delta_rows, token_valid):
    n_i, cols, width = queries.shape
    heads = pair_bias.shape[0]
    size = width // heads
    pairs = n_i // 2
    quads = n_i // 4
    n_rows = lax.axis_size("row")
    parts = lax.axis_size("x")
    keys = parts * cols
    wide = 2 * LANES
    x_at, zl, core = lax.axis_index("x"), lax.axis_index("zl"), lax.axis_index("core")
    place = jnp.stack([zl, core]).astype(jnp.int32)
    valid = lax.dynamic_slice_in_dim(token_valid, ((x_at * 2 + zl) * 2 + core) * cols, cols, 0)
    mask = jnp.where(valid == 1, 0.0, -10000.0).astype(F32)[None]
    struct = jax.ShapeDtypeStruct

    packed = call(
        functools.partial(pack_kernel, math.sqrt(size)),
        "pack",
        struct((heads, 2 * pairs + 1, cols, LANES), BF),
        scratch=[pltpu.VMEM((64, LANES), F32)],
        n_in=7,
    )(queries, keys_values, out_grad, pair_bias, log_norm, delta_rows, mask)
    got = lax.all_to_all(packed, "x", 0, 0, tiled=True)
    own, band = call(
        unpack_kernel,
        "unpack",
        (struct((pairs + 1, keys, LANES), BF), struct((n_rows, cols, wide), BF)),
    )(got)
    swap = [(0, 1), (1, 0)]
    over_core = lax.ppermute(own, "core", swap)
    over_zl = lax.ppermute(own, "zl", swap)
    bias_rows = lax.all_to_all(band, "row", 0, 0, tiled=True)
    over_both = lax.ppermute(over_zl, "core", swap)
    dq, dkv, dbias = call(
        functools.partial(main_kernel, size**-0.5),
        "main",
        (
            struct((4, quads, keys, LANES), BF),
            struct((pairs, keys, LANES), BF),
            struct((n_rows, cols, wide), BF),
        ),
        scratch=[
            pltpu.VMEM((4 * keys, wide), F32),
            pltpu.VMEM((keys, 4 * keys), F32),
            pltpu.VMEM((keys, 4 * keys), F32),
            pltpu.VMEM((n_i * size, 4 * keys), F32),
        ],
        smem=(0,),
        n_in=7,
    )(place, got, own, over_core, over_zl, over_both, bias_rows)
    both = [(0, 3), (1, 2), (2, 1), (3, 0)]
    r1 = lax.ppermute(dq[1], "core", swap)
    r2 = lax.ppermute(dq[2], "zl", swap)
    r3 = lax.ppermute(dq[3], ("zl", "core"), both)
    parts_in = lax.all_to_all(dbias, "row", 0, 0, tiled=True)
    merged = call(
        merge_kernel,
        "merge",
        struct((parts, quads + pairs + 1, cols, LANES), BF),
        n_in=6,
    )(dq[0], r1, r2, r3, dkv, parts_in)
    back = lax.all_to_all(merged, "x", 0, 0, tiled=True)
    query_grad, kv_grad, bias_grad = call(
        final_kernel,
        "final",
        (
            struct((n_i, cols, width), BF),
            struct((cols, n_i, 2 * width), BF),
            struct((heads, cols, cols), F32),
        ),
        scratch=[pltpu.VMEM((cols, 16, 2 * width), F32)],
    )(back)
    return query_grad, kv_grad, bias_grad


def solution(mesh):
    fine = Mesh(mesh.devices.reshape(16, 4, 2, 2), ("row", "x", "zl", "core"))
    col = ("x", "zl", "core")
    placed = (
        P("row", col, None),
        P("row", col, None),
        P("row", col, None),
        P(None, "row", col),
        P(None, "row", col),
        P(None, "row", col),
        P(),
    )
    return jax.shard_map(
        on_device,
        mesh=fine,
        in_specs=placed,
        out_specs=(P("row", col, None), P(col, "row", None), P(None, "row", col)),
        check_vma=False,
    )
```

```python
import functools
import math

import jax
import jax.numpy as jnp
from jax import lax
from jax.experimental import pallas as pl
from jax.experimental.pallas import tpu as pltpu
from jax.sharding import PartitionSpec as P

BF = jnp.bfloat16
F32 = jnp.float32
LANES = 128
HEAD_GROUPS = [[0, 2, 12, 14], [1, 3, 13, 15], [4, 6, 8, 10], [5, 7, 9, 11]]


JOIN_COST = pl.CostEstimate(flops=2_000_000_000, bytes_accessed=1_000_000, transcendentals=0)
SUM_COST = pl.CostEstimate(flops=1_000_000_000, bytes_accessed=1_000_000, transcendentals=0)


def flip(bits):
    return [(c, c ^ bits) for c in range(16)]


def call(body, name, out_shape, scratch=(), n_in=1, space=pltpu.VMEM, limit=48 << 20, cost=None):
    spaces = space if isinstance(space, tuple) else (space,) * n_in
    in_specs = [pl.BlockSpec(memory_space=each) for each in spaces]
    out_specs = jax.tree.map(lambda _: pl.BlockSpec(memory_space=pltpu.VMEM), out_shape)
    return pl.pallas_call(
        body,
        name=name,
        out_shape=out_shape,
        in_specs=in_specs,
        out_specs=out_specs,
        scratch_shapes=list(scratch),
        compiler_params=pltpu.CompilerParams(vmem_limit_bytes=limit),
        cost_estimate=cost,
    )


def place():
    c = lax.axis_index("col")
    x = c // 4
    return c, jnp.bitwise_and(jnp.bitwise_xor(x, x // 2), 1), c % 2


def row_of(b, s):
    _, pair, core = place()
    there = jnp.bitwise_xor(pair, b // 2)
    x = there if s < 2 else 3 - there
    return x * 4 + (s % 2) * 2 + jnp.bitwise_xor(core, b % 2)


def pack_kernel(root, *refs):
    hbm, (out_ref, rows) = refs[:7], refs[7:9]
    local, sems = refs[9:16], refs[16]
    copies = [
        pltpu.make_async_copy(src, dst, sems.at[k])
        for k, (src, dst) in enumerate(zip(hbm, local))
    ]
    for copy in copies:
        copy.start()
    for copy in copies:
        copy.wait()
    q_ref, kv_ref, g_ref, bias_ref, norm_ref, delta_ref, valid_ref = local
    heads, cols, _ = bias_ref.shape
    n_i, _, width = q_ref.shape
    size = width // heads
    pairs = n_i // 2
    count = valid_ref.shape[0]
    valid = jnp.broadcast_to(valid_ref[...].reshape(1, count), (8, count))
    mask = jnp.where(valid == 1, 0.0, -10000.0).astype(F32)
    back = count - place()[0] * cols
    mask = pltpu.roll(mask, back, 1)[0:1, 0:cols]
    for h in range(heads):
        lo, hi = h * size, (h + 1) * size
        for p in range(pairs):
            out_ref[h, p] = jnp.concatenate(
                [
                    q_ref[2 * p, :, lo:hi],
                    g_ref[2 * p, :, lo:hi],
                    q_ref[2 * p + 1, :, lo:hi],
                    g_ref[2 * p + 1, :, lo:hi],
                ],
                axis=-1,
            )
            out_ref[h, pairs + p] = jnp.concatenate(
                [
                    kv_ref[2 * p, :, lo:hi],
                    kv_ref[2 * p, :, width + lo : width + hi],
                    kv_ref[2 * p + 1, :, lo:hi],
                    kv_ref[2 * p + 1, :, width + lo : width + hi],
                ],
                axis=-1,
            )
        rows[...] = jnp.zeros_like(rows)
        norm = norm_ref[:, h, :] * root
        high = norm.astype(BF).astype(F32)
        rows[0:n_i, 0:cols] = high
        rows[16 : 16 + n_i, 0:cols] = norm - high
        delta = delta_ref[:, h, :]
        high = delta.astype(BF).astype(F32)
        rows[32 : 32 + n_i, 0:cols] = high
        rows[48 : 48 + n_i, 0:cols] = delta - high
        turned = jnp.transpose(rows[...])[0:cols]
        tile = bias_ref[h].astype(F32) + mask
        out_ref[h, 2 * pairs] = jnp.concatenate(
            [turned[:, 0:64], tile, jnp.zeros((cols, 64 - cols), F32)], axis=-1
        ).astype(BF)


def own_kernel(got_ref, a_ref):
    parts, blocks, cols, _ = got_ref.shape
    pairs = blocks // 2
    for p in range(pairs):
        a_ref[p] = got_ref[:, p].reshape(parts * cols, LANES)
    a_ref[pairs] = got_ref[:, blocks - 1].reshape(parts * cols, LANES)


def fold(tile):
    tail = tile[:, LANES : LANES + 64]
    return jnp.concatenate(
        [
            tile[:, 0:LANES],
            jnp.concatenate([tail[0:16], tail[16:32]], axis=1),
            jnp.concatenate([tail[32:48], jnp.zeros((16, 64), tile.dtype)], axis=1),
        ],
        axis=0,
    )


def unfold(tile):
    side = tile[48:64]
    tail = jnp.concatenate([side, pltpu.roll(side, 64, 1), tile[64:80]], axis=0)
    return jnp.concatenate([tile[0:48], tail], axis=1)


def band_kernel(got_ref, bias_ref):
    parts, blocks, cols, _ = got_ref.shape
    pieces = [got_ref[x, blocks - 1, :, 64 : 64 + cols].astype(F32) for x in range(parts)]
    band = fold(jnp.concatenate(pieces, axis=-1)).astype(BF)
    for r in range(bias_ref.shape[0]):
        bias_ref[r] = band


def join_kernel(a0_ref, a1_ref, a2_ref, a3_ref, out_ref):
    keys = a0_ref.shape[1]
    for b, a in enumerate((a0_ref, a1_ref, a2_ref, a3_ref)):
        out_ref[:, b * keys : (b + 1) * keys] = a[...]


def main_kernel(
    inv_root,
    got_ref,
    a_ref,
    bias_ref,
    dq0_ref,
    dq2_ref,
    dqc_ref,
    dkv_ref,
    acc,
    rows,
    bias_t,
    dq_t,
):
    parts, blocks, cols, _ = got_ref.shape
    pairs = blocks // 2
    keys = parts * cols
    total = 4 * keys
    size = 32
    log2e = math.log2(math.e)
    dq_refs = (dq0_ref, dqc_ref.at[0], dq2_ref, dqc_ref.at[1])

    for b in range(4):
        for x in range(parts):
            at = b * keys + x * cols
            rows[at : at + cols] = unfold(bias_ref[row_of(b, x)].astype(F32))
    for t in range(0, total, LANES):
        bias_t[:, t : t + LANES] = (
            jnp.transpose(rows[t : t + LANES])[0:keys] * log2e
        )
    acc[...] = jnp.zeros_like(acc)
    lane = lax.broadcasted_iota(jnp.int32, (keys, LANES), 1)
    quarter = lax.broadcasted_iota(jnp.int32, (total, LANES), 1) // size
    extra = a_ref[pairs]
    scale_row = jnp.where((lane // size) % 2 == 0, inv_root, 1.0)
    chunk = 256
    for p in range(pairs):
        qp = a_ref[p]
        qx = jnp.concatenate([qp, extra], axis=1)
        kp = got_ref[:, pairs + p].reshape(keys, LANES)
        kt = jnp.transpose(kp.astype(F32)).astype(BF)
        zero = jnp.zeros_like(kp)
        left = []
        for s in range(4):
            i = 2 * p + s // 2
            base = 32 * (s % 2)
            ones = jnp.where((lane == base + i) | (lane == base + 16 + i), -1.0, 0.0).astype(BF)
            left.append(
                jnp.concatenate([jnp.where(lane // size == s, kp, zero), ones], axis=1)
            )
        qm = [jnp.where(quarter == s, qp, jnp.zeros_like(qp)) for s in range(4)]
        out = jnp.zeros((keys, LANES), F32)
        for t in range(0, total, chunk):
            here = qx[t : t + chunk]
            for e in range(2):
                scores = lax.dot_general(
                    left[2 * e], here, (((1,), (1,)), ((), ())), preferred_element_type=F32
                )
                grads = lax.dot_general(
                    left[2 * e + 1], here, (((1,), (1,)), ((), ())), preferred_element_type=F32
                )
                probs = jnp.exp2(scores * (inv_root * log2e) + bias_t[:, t : t + chunk])
                ds = probs * grads
                acc[:, t : t + chunk] += ds
                ds_low = ds.astype(BF)
                out += jnp.dot(ds_low, qm[2 * e][t : t + chunk], preferred_element_type=F32)
                out += jnp.dot(
                    probs.astype(BF), qm[2 * e + 1][t : t + chunk], preferred_element_type=F32
                )
                i = 2 * p + e
                dq_t[i * size : (i + 1) * size, t : t + chunk] = jnp.dot(
                    kt[2 * e * size : (2 * e + 1) * size], ds_low, preferred_element_type=F32
                )
        dkv_ref[p] = (out * scale_row).astype(BF)
    for quad in range(2 * pairs // 4):
        turned = jnp.transpose(dq_t[quad * LANES : (quad + 1) * LANES]) * inv_root
        for b in range(4):
            dq_refs[b][quad] = turned[b * keys : (b + 1) * keys].astype(BF)


def turn_kernel(cols, acc, dbias_ref, rows):
    keys, total = acc.shape
    for t in range(0, total, LANES):
        rows[t : t + LANES, 0:keys] = jnp.transpose(acc[:, t : t + LANES])
    for b in range(4):
        for x in range(keys // cols):
            at = b * keys + x * cols
            dbias_ref[row_of(b, x)] = fold(rows[at : at + cols]).astype(BF)


def fold_core_kernel(dq0_ref, dq2_ref, got_ref, keep_ref, send_ref):
    keep_ref[...] = dq0_ref[...].astype(F32) + got_ref[0].astype(F32)
    send_ref[...] = (dq2_ref[...].astype(F32) + got_ref[1].astype(F32)).astype(BF)


def sum_kernel(keep_ref, got_ref, out_ref):
    out_ref[...] = (keep_ref[...] + got_ref[...].astype(F32)).astype(BF)


def merge_kernel(total, dkv_ref, db_ref, out_ref):
    parts, _, cols, _ = out_ref.shape
    quads = total.shape[0]
    pairs = dkv_ref.shape[0]
    bias = db_ref[0].astype(F32)
    for r in range(1, db_ref.shape[0]):
        bias = bias + db_ref[r].astype(F32)
    bias = unfold(bias)
    for x in range(parts):
        lo, hi = x * cols, (x + 1) * cols
        for quad in range(quads):
            out_ref[x, quad] = total[quad, lo:hi]
        for p in range(pairs):
            out_ref[x, quads + p] = dkv_ref[p, lo:hi]
        out_ref[x, quads + pairs] = jnp.concatenate(
            [bias[:, lo:hi], jnp.zeros((cols, LANES - cols), F32)], axis=-1
        ).astype(BF)


def final_kernel(got_ref, dq_ref, dkv_ref, db_ref):
    heads, blocks, cols, _ = got_ref.shape
    size = 32
    n_i = dq_ref.shape[0]
    quads = n_i // 4
    for i in range(n_i):
        at = (i % 4) * size
        dq_ref[i] = jnp.concatenate(
            [got_ref[h, i // 4, :, at : at + size] for h in range(heads)], axis=-1
        )
        at = (i % 2) * 2 * size
        dkv_ref[i] = jnp.concatenate(
            [got_ref[h, quads + i // 2, :, at : at + size] for h in range(heads)]
            + [got_ref[h, quads + i // 2, :, at + size : at + 2 * size] for h in range(heads)],
            axis=-1,
        )
    for h in range(heads):
        db_ref[h] = got_ref[h, blocks - 1, :, 0:cols].astype(F32)


def on_device(queries, keys_values, out_grad, pair_bias, log_norm, delta_rows, token_valid):
    n_i, cols, width = queries.shape
    heads = pair_bias.shape[0]
    size = width // heads
    pairs = n_i // 2
    quads = n_i // 4
    n_rows = lax.axis_size("row")
    parts = heads
    keys = parts * cols
    wide = 2 * LANES
    struct = jax.ShapeDtypeStruct
    inputs = (
        queries,
        keys_values,
        out_grad,
        pair_bias,
        jnp.transpose(log_norm, (1, 0, 2)),
        jnp.transpose(delta_rows, (1, 0, 2)),
        token_valid,
    )

    packed = call(
        functools.partial(pack_kernel, math.sqrt(size)),
        "pack",
        struct((heads, 2 * pairs + 1, cols, LANES), BF),
        scratch=[pltpu.VMEM((64, LANES), F32)]
        + [pltpu.VMEM(v.shape, v.dtype) for v in inputs]
        + [pltpu.SemaphoreType.DMA((len(inputs),))],
        n_in=len(inputs),
        space=pltpu.HBM,
        limit=62 << 20,
    )(*inputs)
    got = lax.all_to_all(packed, "col", 0, 0, tiled=True, axis_index_groups=HEAD_GROUPS)
    own = call(own_kernel, "own", struct((pairs + 1, keys, LANES), BF))(got)
    over_x = lax.ppermute(own, "col", flip(4))
    over_core = lax.ppermute(own, "col", flip(1))
    folded = struct((n_rows, 80, LANES), BF)
    dq_block = struct((quads, keys, LANES), BF)
    band = call(band_kernel, "band", folded)(got)
    bias_rows = lax.all_to_all(band, "row", 0, 0, tiled=True)
    over_both = lax.ppermute(over_x, "col", flip(1))
    joined = call(
        join_kernel,
        "join",
        struct((pairs + 1, 4 * keys, LANES), BF),
        n_in=4,
        cost=JOIN_COST,
    )(own, over_core, over_x, over_both)
    dq0, dq2, dq_core, dkv, acc = call(
        functools.partial(main_kernel, size**-0.5),
        "main",
        (
            dq_block,
            dq_block,
            struct((2, quads, keys, LANES), BF),
            struct((pairs, keys, LANES), BF),
            struct((keys, 4 * keys), F32),
        ),
        scratch=[
            pltpu.VMEM((4 * keys, wide), F32),
            pltpu.VMEM((keys, 4 * keys), F32),
            pltpu.VMEM((n_i * size, 4 * keys), F32),
        ],
        n_in=3,
    )(got, joined, bias_rows)
    over_core = lax.ppermute(dq_core, "col", flip(1))
    dbias = call(
        functools.partial(turn_kernel, cols),
        "turn",
        folded,
        scratch=[pltpu.VMEM((4 * keys, wide), F32)],
    )(acc)
    keep, send = call(
        fold_core_kernel,
        "fold_core",
        (struct((quads, keys, LANES), F32), dq_block),
        n_in=3,
    )(dq0, dq2, over_core)
    over_x = lax.ppermute(send, "col", flip(4))
    parts_in = lax.all_to_all(dbias, "row", 0, 0, tiled=True)
    total = call(sum_kernel, "sum", dq_block, n_in=2, cost=SUM_COST)(keep, over_x)
    merged = call(
        merge_kernel,
        "merge",
        struct((parts, quads + pairs + 1, cols, LANES), BF),
        n_in=3,
    )(total, dkv, parts_in)
    back = lax.all_to_all(merged, "col", 0, 0, tiled=True, axis_index_groups=HEAD_GROUPS)
    query_grad, kv_grad, bias_grad = call(
        final_kernel,
        "final",
        (
            struct((n_i, cols, width), BF),
            struct((n_i, cols, 2 * width), BF),
            struct((heads, cols, cols), F32),
        ),
    )(back)
    kv_grad = jnp.transpose(kv_grad, (1, 0, 2))
    return query_grad, kv_grad, bias_grad


def solution(mesh):
    placed = (
        P("row", "col", None),
        P("row", "col", None),
        P("row", "col", None),
        P(None, "row", "col"),
        P(None, "row", "col"),
        P(None, "row", "col"),
        P(),
    )
    return jax.shard_map(
        on_device,
        mesh=mesh,
        in_specs=placed,
        out_specs=(P("row", "col", None), P("col", "row", None), P(None, "row", "col")),
        check_vma=False,
    )
```

```python
import functools
import math

import jax
import jax.numpy as jnp
from jax import lax
from jax.experimental import pallas as pl
from jax.experimental.pallas import tpu as pltpu
from jax.sharding import PartitionSpec as P

BF = jnp.bfloat16
F32 = jnp.float32
LANES = 128
HEAD_GROUPS = [[0, 2, 12, 14], [1, 3, 13, 15], [4, 6, 8, 10], [5, 7, 9, 11]]


JOIN_COST = pl.CostEstimate(flops=2_000_000_000, bytes_accessed=1_000_000, transcendentals=0)
SUM_COST = pl.CostEstimate(flops=1_000_000_000, bytes_accessed=1_000_000, transcendentals=0)


def flip(bits):
    return [(c, c ^ bits) for c in range(16)]


def trade(step):
    return [(group[p], group[p ^ step]) for group in HEAD_GROUPS for p in range(4)]


def call(body, name, out_shape, scratch=(), n_in=1, space=pltpu.VMEM, limit=48 << 20, cost=None):
    spaces = space if isinstance(space, tuple) else (space,) * n_in
    in_specs = [pl.BlockSpec(memory_space=each) for each in spaces]
    out_specs = jax.tree.map(lambda _: pl.BlockSpec(memory_space=pltpu.VMEM), out_shape)
    return pl.pallas_call(
        body,
        name=name,
        out_shape=out_shape,
        in_specs=in_specs,
        out_specs=out_specs,
        scratch_shapes=list(scratch),
        compiler_params=pltpu.CompilerParams(vmem_limit_bytes=limit),
        cost_estimate=cost,
    )


def place():
    c = lax.axis_index("col")
    x = c // 4
    pair = jnp.bitwise_and(jnp.bitwise_xor(x, x // 2), 1)
    return c, pair, c % 2, (x // 2) * 2 + (c // 2) % 2


def row_of(b, step):
    _, pair, core, position = place()
    there = jnp.bitwise_xor(pair, b // 2)
    to = jnp.bitwise_xor(position, step)
    x = jnp.where(to >= 2, 3 - there, there)
    return x * 4 + (to % 2) * 2 + jnp.bitwise_xor(core, b % 2)


def pack_kernel(root, *refs):
    hbm, out_refs, staged, rows = refs[:7], refs[7:11], refs[11], refs[12]
    local, sems = refs[13:20], refs[20]
    copies = [
        pltpu.make_async_copy(src, dst, sems.at[k])
        for k, (src, dst) in enumerate(zip(hbm, local))
    ]
    for copy in copies:
        copy.start()
    for copy in copies:
        copy.wait()
    q_ref, kv_ref, g_ref, bias_ref, norm_ref, delta_ref, valid_ref = local
    heads, cols, _ = bias_ref.shape
    n_i, _, width = q_ref.shape
    size = width // heads
    pairs = n_i // 2
    count = valid_ref.shape[0]
    valid = jnp.broadcast_to(valid_ref[...].reshape(1, count), (8, count))
    mask = jnp.where(valid == 1, 0.0, -10000.0).astype(F32)
    c, _, _, position = place()
    back = count - c * cols
    mask = pltpu.roll(mask, back, 1)[0:1, 0:cols]
    for h in range(heads):
        lo, hi = h * size, (h + 1) * size
        to = jnp.bitwise_xor(position, h)
        for p in range(pairs):
            staged[to, p] = jnp.concatenate(
                [
                    q_ref[2 * p, :, lo:hi],
                    g_ref[2 * p, :, lo:hi],
                    q_ref[2 * p + 1, :, lo:hi],
                    g_ref[2 * p + 1, :, lo:hi],
                ],
                axis=-1,
            )
            staged[to, pairs + p] = jnp.concatenate(
                [
                    kv_ref[2 * p, :, lo:hi],
                    kv_ref[2 * p, :, width + lo : width + hi],
                    kv_ref[2 * p + 1, :, lo:hi],
                    kv_ref[2 * p + 1, :, width + lo : width + hi],
                ],
                axis=-1,
            )
        rows[...] = jnp.zeros_like(rows)
        norm = norm_ref[:, h, :] * root
        high = norm.astype(BF).astype(F32)
        rows[0:n_i, 0:cols] = high
        rows[16 : 16 + n_i, 0:cols] = norm - high
        delta = delta_ref[:, h, :]
        high = delta.astype(BF).astype(F32)
        rows[32 : 32 + n_i, 0:cols] = high
        rows[48 : 48 + n_i, 0:cols] = delta - high
        turned = jnp.transpose(rows[...])[0:cols]
        tile = bias_ref[h].astype(F32) + mask
        staged[to, 2 * pairs] = jnp.concatenate(
            [turned[:, 0:64], tile, jnp.zeros((cols, 64 - cols), F32)], axis=-1
        ).astype(BF)
    for step in range(heads):
        out_refs[step][...] = staged[step]


def hold_kernel(src_ref, out_ref, sem):
    copy = pltpu.make_async_copy(src_ref, out_ref, sem)
    copy.start()
    copy.wait()


def own_kernel(*refs):
    got, own_ref = refs[0:4], refs[4]
    blocks, cols, _ = got[0].shape
    pairs = blocks // 2
    for step in range(4):
        lo, hi = step * cols, (step + 1) * cols
        own_ref[0:pairs, lo:hi] = got[step][0:pairs]
        own_ref[pairs, lo:hi] = got[step][blocks - 1]


def fold(tile):
    tail = tile[:, LANES : LANES + 64]
    return jnp.concatenate(
        [
            tile[:, 0:LANES],
            jnp.concatenate([tail[0:16], tail[16:32]], axis=1),
            jnp.concatenate([tail[32:48], jnp.zeros((16, 64), tile.dtype)], axis=1),
        ],
        axis=0,
    )


def unfold(tile):
    side = tile[48:64]
    tail = jnp.concatenate([side, pltpu.roll(side, 64, 1), tile[64:80]], axis=0)
    return jnp.concatenate([tile[0:48], tail], axis=1)


def band_kernel(*refs):
    got, bias_ref = refs[0:4], refs[4]
    blocks, cols, _ = got[0].shape
    tiles = [one[blocks - 1, :, 64 : 64 + cols].astype(F32) for one in got]
    band = fold(jnp.concatenate(tiles, axis=-1))
    for r in range(bias_ref.shape[0]):
        bias_ref[r] = band.astype(BF)


def join_kernel(a0_ref, a1_ref, a2_ref, a3_ref, out_ref):
    keys = a0_ref.shape[1]
    for b, a in enumerate((a0_ref, a1_ref, a2_ref, a3_ref)):
        out_ref[:, b * keys : (b + 1) * keys] = a[...]


def main_kernel(inv_root, *refs):
    ab_refs, a_ref, bias_ref = refs[0:4], refs[4], refs[5]
    dq0_ref, dq2_ref, dqc_ref, dkv_ref, dbias_ref = refs[6:11]
    rows, bias_t, acc, dq_t = refs[11:]
    blocks, cols, _ = ab_refs[0].shape
    parts = len(ab_refs)
    pairs = blocks // 2
    keys = parts * cols
    total = 4 * keys
    size = 32
    log2e = math.log2(math.e)
    dq_refs = (dq0_ref, dqc_ref.at[0], dq2_ref, dqc_ref.at[1])
    for b in range(4):
        for x in range(parts):
            at = b * keys + x * cols
            rows[at : at + cols] = unfold(bias_ref[row_of(b, x)].astype(F32))
    for t in range(0, total, LANES):
        bias_t[:, t : t + LANES] = (
            jnp.transpose(rows[t : t + LANES])[0:keys] * log2e
        )
    acc[...] = jnp.zeros_like(acc)
    lane = lax.broadcasted_iota(jnp.int32, (keys, LANES), 1)
    quarter = lax.broadcasted_iota(jnp.int32, (total, LANES), 1) // size
    extra = a_ref[pairs]
    scale_row = jnp.where((lane // size) % 2 == 0, inv_root, 1.0)
    for p in range(pairs):
        qp = a_ref[p]
        qx = jnp.concatenate([qp, extra], axis=1)
        kp = jnp.concatenate([ab[pairs + p] for ab in ab_refs], axis=0)
        kt = jnp.transpose(kp.astype(F32)).astype(BF)
        zero = jnp.zeros_like(kp)
        left = []
        for s in range(4):
            i = 2 * p + s // 2
            base = 32 * (s % 2)
            ones = jnp.where((lane == base + i) | (lane == base + 16 + i), -1.0, 0.0).astype(BF)
            left.append(
                jnp.concatenate([jnp.where(lane // size == s, kp, zero), ones], axis=1)
            )
        low = []
        for e in range(2):
            both = lax.dot_general(
                jnp.concatenate(left[2 * e : 2 * e + 2], axis=0),
                qx,
                (((1,), (1,)), ((), ())),
                preferred_element_type=F32,
            )
            probs = jnp.exp2(both[0:keys] * (inv_root * log2e) + bias_t[...])
            ds = probs * both[keys:]
            acc[...] += ds
            low += [ds.astype(BF), probs.astype(BF)]
            i = 2 * p + e
            dq_t[i * size : (i + 1) * size] = jnp.dot(
                kt[2 * e * size : (2 * e + 1) * size], low[2 * e], preferred_element_type=F32
            )
        out = jnp.zeros((keys, LANES), F32)
        for s in range(4):
            out += jnp.dot(
                low[s], jnp.where(quarter == s, qp, jnp.zeros_like(qp)), preferred_element_type=F32
            )
        dkv_ref[p] = (out * scale_row).astype(BF)
    for quad in range(2 * pairs // 4):
        turned = jnp.transpose(dq_t[quad * LANES : (quad + 1) * LANES]) * inv_root
        for b in range(4):
            dq_refs[b][quad] = turned[b * keys : (b + 1) * keys].astype(BF)
    for t in range(0, total, LANES):
        rows[t : t + LANES, 0:keys] = jnp.transpose(acc[:, t : t + LANES])
    for b in range(4):
        for x in range(parts):
            at = b * keys + x * cols
            dbias_ref[row_of(b, x)] = fold(rows[at : at + cols]).astype(BF)


def fold_core_kernel(dq0_ref, dq2_ref, got_ref, keep_ref, send_ref):
    keep_ref[...] = dq0_ref[...].astype(F32) + got_ref[0].astype(F32)
    send_ref[...] = (dq2_ref[...].astype(F32) + got_ref[1].astype(F32)).astype(BF)


def sum_kernel(keep_ref, got_ref, out_ref):
    out_ref[...] = (keep_ref[...] + got_ref[...].astype(F32)).astype(BF)


def merge_kernel(total, dkv_ref, db_ref, out_ref):
    parts, _, cols, _ = out_ref.shape
    quads = total.shape[0]
    pairs = dkv_ref.shape[0]
    bias = db_ref[0].astype(F32)
    for r in range(1, db_ref.shape[0]):
        bias = bias + db_ref[r].astype(F32)
    bias = unfold(bias)
    position = place()[3]
    for step in range(parts):
        x = jnp.bitwise_xor(position, step)
        lo, hi = step * cols, (step + 1) * cols
        for quad in range(quads):
            out_ref[x, quad] = total[quad, lo:hi]
        for p in range(pairs):
            out_ref[x, quads + p] = dkv_ref[p, lo:hi]
        out_ref[x, quads + pairs] = jnp.concatenate(
            [bias[:, lo:hi], jnp.zeros((cols, LANES - cols), F32)], axis=-1
        ).astype(BF)


def final_kernel(got_ref, dq_ref, dkv_ref, db_ref):
    heads, blocks, cols, _ = got_ref.shape
    size = 32
    n_i = dq_ref.shape[0]
    quads = n_i // 4
    for i in range(n_i):
        at = (i % 4) * size
        dq_ref[i] = jnp.concatenate(
            [got_ref[h, i // 4, :, at : at + size] for h in range(heads)], axis=-1
        )
        at = (i % 2) * 2 * size
        dkv_ref[i] = jnp.concatenate(
            [got_ref[h, quads + i // 2, :, at : at + size] for h in range(heads)]
            + [got_ref[h, quads + i // 2, :, at + size : at + 2 * size] for h in range(heads)],
            axis=-1,
        )
    for h in range(heads):
        db_ref[h] = got_ref[h, blocks - 1, :, 0:cols].astype(F32)


def on_device(queries, keys_values, out_grad, pair_bias, log_norm, delta_rows, token_valid):
    n_i, cols, width = queries.shape
    heads = pair_bias.shape[0]
    size = width // heads
    pairs = n_i // 2
    quads = n_i // 4
    n_rows = lax.axis_size("row")
    keys = heads * cols
    wide = 2 * LANES
    struct = jax.ShapeDtypeStruct
    inputs = (
        queries,
        keys_values,
        out_grad,
        pair_bias,
        jnp.transpose(log_norm, (1, 0, 2)),
        jnp.transpose(delta_rows, (1, 0, 2)),
        token_valid,
    )

    def traded(blocks):
        return [blocks[0]] + [lax.ppermute(blocks[k], "col", trade(k)) for k in (1, 2, 3)]

    sent = call(
        functools.partial(pack_kernel, math.sqrt(size)),
        "pack",
        (struct((2 * pairs + 1, cols, LANES), BF),) * 4,
        scratch=[
            pltpu.VMEM((heads, 2 * pairs + 1, cols, LANES), BF),
            pltpu.VMEM((64, LANES), F32),
        ]
        + [pltpu.VMEM(v.shape, v.dtype) for v in inputs]
        + [pltpu.SemaphoreType.DMA((len(inputs),))],
        n_in=len(inputs),
        space=pltpu.HBM,
        limit=62 << 20,
    )(*inputs)
    held = call(
        hold_kernel,
        "hold",
        struct(sent[0].shape, BF),
        scratch=[pltpu.SemaphoreType.DMA],
        space=pltpu.HBM,
    )(sent[0])
    blocks = [held] + traded(sent)[1:]
    own = call(own_kernel, "own", struct((pairs + 1, keys, LANES), BF), n_in=4)(*blocks)
    over_x = lax.ppermute(own, "col", flip(4))
    over_core = lax.ppermute(own, "col", flip(1))
    folded = struct((n_rows, 80, LANES), BF)
    dq_block = struct((quads, keys, LANES), BF)
    band = call(band_kernel, "band", folded, n_in=4)(*blocks)
    bias_rows = lax.all_to_all(band, "row", 0, 0, tiled=True)
    over_both = lax.ppermute(over_x, "col", flip(1))
    joined = call(
        join_kernel,
        "join",
        struct((pairs + 1, 4 * keys, LANES), BF),
        n_in=4,
        cost=JOIN_COST,
    )(own, over_core, over_x, over_both)
    dq0, dq2, dq_core, dkv, dbias = call(
        functools.partial(main_kernel, size**-0.5),
        "main",
        (
            dq_block,
            dq_block,
            struct((2, quads, keys, LANES), BF),
            struct((pairs, keys, LANES), BF),
            folded,
        ),
        scratch=[
            pltpu.VMEM((4 * keys, wide), F32),
            pltpu.VMEM((keys, 4 * keys), F32),
            pltpu.VMEM((keys, 4 * keys), F32),
            pltpu.VMEM((n_i * size, 4 * keys), F32),
        ],
        n_in=6,
    )(*blocks, joined, bias_rows)
    over_core = lax.ppermute(dq_core, "col", flip(1))
    keep, send = call(
        fold_core_kernel,
        "fold_core",
        (struct((quads, keys, LANES), F32), dq_block),
        n_in=3,
    )(dq0, dq2, over_core)
    over_x = lax.ppermute(send, "col", flip(4))
    parts_in = lax.all_to_all(dbias, "row", 0, 0, tiled=True)
    total = call(sum_kernel, "sum", dq_block, n_in=2, cost=SUM_COST)(keep, over_x)
    merged = call(
        merge_kernel,
        "merge",
        struct((heads, quads + pairs + 1, cols, LANES), BF),
        n_in=3,
    )(total, dkv, parts_in)
    back = lax.all_to_all(merged, "col", 0, 0, tiled=True, axis_index_groups=HEAD_GROUPS)
    query_grad, kv_grad, bias_grad = call(
        final_kernel,
        "final",
        (
            struct((n_i, cols, width), BF),
            struct((n_i, cols, 2 * width), BF),
            struct((heads, cols, cols), F32),
        ),
    )(back)
    kv_grad = jnp.transpose(kv_grad, (1, 0, 2))
    return query_grad, kv_grad, bias_grad


def solution(mesh):
    placed = (
        P("row", "col", None),
        P("row", "col", None),
        P("row", "col", None),
        P(None, "row", "col"),
        P(None, "row", "col"),
        P(None, "row", "col"),
        P(),
    )
    return jax.shard_map(
        on_device,
        mesh=mesh,
        in_specs=placed,
        out_specs=(P("row", "col", None), P("col", "row", None), P(None, "row", "col")),
        check_vma=False,
    )
```

```python
import functools
import math

import jax
import jax.numpy as jnp
from jax import lax
from jax.experimental import pallas as pl
from jax.experimental.pallas import tpu as pltpu
from jax.sharding import PartitionSpec as P

BF = jnp.bfloat16
F32 = jnp.float32
LANES = 128
HEAD_GROUPS = [[0, 2, 12, 14], [1, 3, 13, 15], [4, 6, 8, 10], [5, 7, 9, 11]]


JOIN_COST = pl.CostEstimate(flops=2_000_000_000, bytes_accessed=1_000_000, transcendentals=0)
SUM_COST = pl.CostEstimate(flops=1_000_000_000, bytes_accessed=1_000_000, transcendentals=0)


def flip(bits):
    return [(c, c ^ bits) for c in range(16)]


def trade(step):
    return [(group[p], group[p ^ step]) for group in HEAD_GROUPS for p in range(4)]


def call(body, name, out_shape, scratch=(), n_in=1, space=pltpu.VMEM, limit=48 << 20, cost=None):
    spaces = space if isinstance(space, tuple) else (space,) * n_in
    in_specs = [pl.BlockSpec(memory_space=each) for each in spaces]
    out_specs = jax.tree.map(lambda _: pl.BlockSpec(memory_space=pltpu.VMEM), out_shape)
    return pl.pallas_call(
        body,
        name=name,
        out_shape=out_shape,
        in_specs=in_specs,
        out_specs=out_specs,
        scratch_shapes=list(scratch),
        compiler_params=pltpu.CompilerParams(vmem_limit_bytes=limit),
        cost_estimate=cost,
    )


def place():
    c = lax.axis_index("col")
    x = c // 4
    pair = jnp.bitwise_and(jnp.bitwise_xor(x, x // 2), 1)
    return c, pair, c % 2, (x // 2) * 2 + (c // 2) % 2


def row_of(b, step):
    _, pair, core, position = place()
    there = jnp.bitwise_xor(pair, b // 2)
    to = jnp.bitwise_xor(position, step)
    x = jnp.where(to >= 2, 3 - there, there)
    return x * 4 + (to % 2) * 2 + jnp.bitwise_xor(core, b % 2)


def pack_kernel(root, *refs):
    hbm, out_refs, staged, rows = refs[:7], refs[7:11], refs[11], refs[12]
    local, sems = refs[13:20], refs[20]
    copies = [
        pltpu.make_async_copy(src, dst, sems.at[k])
        for k, (src, dst) in enumerate(zip(hbm, local))
    ]
    for copy in copies:
        copy.start()
    for copy in copies:
        copy.wait()
    q_ref, kv_ref, g_ref, bias_ref, norm_ref, delta_ref, valid_ref = local
    heads, cols, _ = bias_ref.shape
    n_i, _, width = q_ref.shape
    size = width // heads
    pairs = n_i // 2
    count = valid_ref.shape[0]
    valid = jnp.broadcast_to(valid_ref[...].reshape(1, count), (8, count))
    mask = jnp.where(valid == 1, 0.0, -10000.0).astype(F32)
    c, _, _, position = place()
    back = count - c * cols
    mask = pltpu.roll(mask, back, 1)[0:1, 0:cols]
    for h in range(heads):
        lo, hi = h * size, (h + 1) * size
        to = jnp.bitwise_xor(position, h)
        for p in range(pairs):
            staged[to, p] = jnp.concatenate(
                [
                    q_ref[2 * p, :, lo:hi],
                    g_ref[2 * p, :, lo:hi],
                    q_ref[2 * p + 1, :, lo:hi],
                    g_ref[2 * p + 1, :, lo:hi],
                ],
                axis=-1,
            )
            staged[to, pairs + p] = jnp.concatenate(
                [
                    kv_ref[2 * p, :, lo:hi],
                    kv_ref[2 * p, :, width + lo : width + hi],
                    kv_ref[2 * p + 1, :, lo:hi],
                    kv_ref[2 * p + 1, :, width + lo : width + hi],
                ],
                axis=-1,
            )
        rows[...] = jnp.zeros_like(rows)
        norm = norm_ref[:, h, :] * root
        high = norm.astype(BF).astype(F32)
        rows[0:n_i, 0:cols] = high
        rows[16 : 16 + n_i, 0:cols] = norm - high
        delta = delta_ref[:, h, :]
        high = delta.astype(BF).astype(F32)
        rows[32 : 32 + n_i, 0:cols] = high
        rows[48 : 48 + n_i, 0:cols] = delta - high
        turned = jnp.transpose(rows[...])[0:cols]
        tile = bias_ref[h].astype(F32) + mask
        staged[to, 2 * pairs] = jnp.concatenate(
            [turned[:, 0:64], tile, jnp.zeros((cols, 64 - cols), F32)], axis=-1
        ).astype(BF)
    for step in range(heads):
        out_refs[step][...] = staged[step]


def hold_kernel(src_ref, out_ref, sem):
    copy = pltpu.make_async_copy(src_ref, out_ref, sem)
    copy.start()
    copy.wait()


def own_kernel(*refs):
    got, own_ref = refs[0:4], refs[4]
    blocks, cols, _ = got[0].shape
    pairs = blocks // 2
    for step in range(4):
        lo, hi = step * cols, (step + 1) * cols
        own_ref[0:pairs, lo:hi] = got[step][0:pairs]
        own_ref[pairs, lo:hi] = got[step][blocks - 1]


def fold(tile):
    tail = tile[:, LANES : LANES + 64]
    return jnp.concatenate(
        [
            tile[:, 0:LANES],
            jnp.concatenate([tail[0:16], tail[16:32]], axis=1),
            jnp.concatenate([tail[32:48], jnp.zeros((16, 64), tile.dtype)], axis=1),
        ],
        axis=0,
    )


def unfold(tile):
    side = tile[48:64]
    tail = jnp.concatenate([side, pltpu.roll(side, 64, 1), tile[64:80]], axis=0)
    return jnp.concatenate([tile[0:48], tail], axis=1)


def band_kernel(*refs):
    got, bias_ref = refs[0:4], refs[4]
    blocks, cols, _ = got[0].shape
    tiles = [one[blocks - 1, :, 64 : 64 + cols].astype(F32) for one in got]
    band = fold(jnp.concatenate(tiles, axis=-1))
    for r in range(bias_ref.shape[0]):
        bias_ref[r] = band.astype(BF)


def join_kernel(a0_ref, a1_ref, a2_ref, a3_ref, out_ref):
    keys = a0_ref.shape[1]
    for b, a in enumerate((a0_ref, a1_ref, a2_ref, a3_ref)):
        out_ref[:, b * keys : (b + 1) * keys] = a[...]


def main_kernel(inv_root, *refs):
    ab_refs, a_ref, bias_ref = refs[0:4], refs[4], refs[5]
    dq0_ref, dq2_ref, dqc_ref = refs[6:9]
    dkv_refs, dbias_ref = refs[9:13], refs[13]
    rows, bias_t, acc, dq_t = refs[14:]
    blocks, cols, _ = ab_refs[0].shape
    parts = len(ab_refs)
    pairs = blocks // 2
    keys = parts * cols
    total = 4 * keys
    size = 32
    log2e = math.log2(math.e)
    dq_refs = (dq0_ref, dqc_ref.at[0], dq2_ref, dqc_ref.at[1])
    for b in range(4):
        for x in range(parts):
            at = b * keys + x * cols
            rows[at : at + cols] = unfold(bias_ref[row_of(b, x)].astype(F32))
    for t in range(0, total, LANES):
        bias_t[:, t : t + LANES] = (
            jnp.transpose(rows[t : t + LANES])[0:keys] * log2e
        )
    acc[...] = jnp.zeros_like(acc)
    lane = lax.broadcasted_iota(jnp.int32, (keys, LANES), 1)
    quarter = lax.broadcasted_iota(jnp.int32, (total, LANES), 1) // size
    extra = a_ref[pairs]
    scale_row = jnp.where((lane // size) % 2 == 0, inv_root, 1.0)
    for p in range(pairs):
        qp = a_ref[p]
        qx = jnp.concatenate([qp, extra], axis=1)
        kp = jnp.concatenate([ab[pairs + p] for ab in ab_refs], axis=0)
        kt = jnp.transpose(kp.astype(F32)).astype(BF)
        zero = jnp.zeros_like(kp)
        left = []
        for s in range(4):
            i = 2 * p + s // 2
            base = 32 * (s % 2)
            ones = jnp.where((lane == base + i) | (lane == base + 16 + i), -1.0, 0.0).astype(BF)
            left.append(
                jnp.concatenate([jnp.where(lane // size == s, kp, zero), ones], axis=1)
            )
        low = []
        for e in range(2):
            both = lax.dot_general(
                jnp.concatenate(left[2 * e : 2 * e + 2], axis=0),
                qx,
                (((1,), (1,)), ((), ())),
                preferred_element_type=F32,
            )
            probs = jnp.exp2(both[0:keys] * (inv_root * log2e) + bias_t[...])
            ds = probs * both[keys:]
            acc[...] += ds
            low += [ds.astype(BF), probs.astype(BF)]
            i = 2 * p + e
            dq_t[i * size : (i + 1) * size] = jnp.dot(
                kt[2 * e * size : (2 * e + 1) * size], low[2 * e], preferred_element_type=F32
            )
        out = jnp.zeros((keys, LANES), F32)
        for s in range(4):
            out += jnp.dot(
                low[s], jnp.where(quarter == s, qp, jnp.zeros_like(qp)), preferred_element_type=F32
            )
        out = (out * scale_row).astype(BF)
        for step in range(parts):
            dkv_refs[step][p] = out[step * cols : (step + 1) * cols]
    for quad in range(2 * pairs // 4):
        turned = jnp.transpose(dq_t[quad * LANES : (quad + 1) * LANES]) * inv_root
        for b in range(4):
            dq_refs[b][quad] = turned[b * keys : (b + 1) * keys].astype(BF)
    for t in range(0, total, LANES):
        rows[t : t + LANES, 0:keys] = jnp.transpose(acc[:, t : t + LANES])
    for b in range(4):
        for x in range(parts):
            at = b * keys + x * cols
            dbias_ref[row_of(b, x)] = fold(rows[at : at + cols]).astype(BF)


def fold_core_kernel(dq0_ref, dq2_ref, got_ref, keep_ref, send_ref):
    keep_ref[...] = dq0_ref[...].astype(F32) + got_ref[0].astype(F32)
    send_ref[...] = (dq2_ref[...].astype(F32) + got_ref[1].astype(F32)).astype(BF)


def sum_kernel(keep_ref, got_ref, out_ref):
    out_ref[...] = (keep_ref[...] + got_ref[...].astype(F32)).astype(BF)


def merge_kernel(total, db_ref, *out_refs):
    quads = total.shape[0]
    cols = out_refs[0].shape[1]
    bias = db_ref[0].astype(F32)
    for r in range(1, db_ref.shape[0]):
        bias = bias + db_ref[r].astype(F32)
    bias = unfold(bias)
    for step, out_ref in enumerate(out_refs):
        lo, hi = step * cols, (step + 1) * cols
        out_ref[0:quads] = total[:, lo:hi]
        out_ref[quads] = jnp.concatenate(
            [bias[:, lo:hi], jnp.zeros((cols, LANES - cols), F32)], axis=-1
        ).astype(BF)


def final_kernel(*refs):
    f_refs, kv_refs = refs[0:4], refs[4:8]
    dq_ref, dkv_ref, db_ref, f_all, kv_all = refs[8:]
    heads, cols = len(f_refs), dq_ref.shape[1]
    size = 32
    n_i = dq_ref.shape[0]
    quads = n_i // 4
    position = place()[3]
    for step in range(heads):
        h = jnp.bitwise_xor(position, step)
        f_all[h] = f_refs[step][...]
        kv_all[h] = kv_refs[step][...]
    for i in range(n_i):
        at = (i % 4) * size
        dq_ref[i] = jnp.concatenate(
            [f_all[h, i // 4, :, at : at + size] for h in range(heads)], axis=-1
        )
        at = (i % 2) * 2 * size
        dkv_ref[i] = jnp.concatenate(
            [kv_all[h, i // 2, :, at : at + size] for h in range(heads)]
            + [kv_all[h, i // 2, :, at + size : at + 2 * size] for h in range(heads)],
            axis=-1,
        )
    for h in range(heads):
        db_ref[h] = f_all[h, quads, :, 0:cols].astype(F32)


def on_device(queries, keys_values, out_grad, pair_bias, log_norm, delta_rows, token_valid):
    n_i, cols, width = queries.shape
    heads = pair_bias.shape[0]
    size = width // heads
    pairs = n_i // 2
    quads = n_i // 4
    n_rows = lax.axis_size("row")
    keys = heads * cols
    wide = 2 * LANES
    struct = jax.ShapeDtypeStruct
    inputs = (
        queries,
        keys_values,
        out_grad,
        pair_bias,
        jnp.transpose(log_norm, (1, 0, 2)),
        jnp.transpose(delta_rows, (1, 0, 2)),
        token_valid,
    )

    def traded(blocks):
        return [blocks[0]] + [lax.ppermute(blocks[k], "col", trade(k)) for k in (1, 2, 3)]

    sent = call(
        functools.partial(pack_kernel, math.sqrt(size)),
        "pack",
        (struct((2 * pairs + 1, cols, LANES), BF),) * 4,
        scratch=[
            pltpu.VMEM((heads, 2 * pairs + 1, cols, LANES), BF),
            pltpu.VMEM((64, LANES), F32),
        ]
        + [pltpu.VMEM(v.shape, v.dtype) for v in inputs]
        + [pltpu.SemaphoreType.DMA((len(inputs),))],
        n_in=len(inputs),
        space=pltpu.HBM,
        limit=62 << 20,
    )(*inputs)
    held = call(
        hold_kernel,
        "hold",
        struct(sent[0].shape, BF),
        scratch=[pltpu.SemaphoreType.DMA],
        space=pltpu.HBM,
    )(sent[0])
    blocks = [held] + traded(sent)[1:]
    own = call(own_kernel, "own", struct((pairs + 1, keys, LANES), BF), n_in=4)(*blocks)
    over_x = lax.ppermute(own, "col", flip(4))
    over_core = lax.ppermute(own, "col", flip(1))
    folded = struct((n_rows, 80, LANES), BF)
    dq_block = struct((quads, keys, LANES), BF)
    band = call(band_kernel, "band", folded, n_in=4)(*blocks)
    bias_rows = lax.all_to_all(band, "row", 0, 0, tiled=True)
    over_both = lax.ppermute(over_x, "col", flip(1))
    joined = call(
        join_kernel,
        "join",
        struct((pairs + 1, 4 * keys, LANES), BF),
        n_in=4,
        cost=JOIN_COST,
    )(own, over_core, over_x, over_both)
    dq0, dq2, dq_core, *dkv, dbias = call(
        functools.partial(main_kernel, size**-0.5),
        "main",
        (
            dq_block,
            dq_block,
            struct((2, quads, keys, LANES), BF),
        )
        + (struct((pairs, cols, LANES), BF),) * 4
        + (folded,),
        scratch=[
            pltpu.VMEM((4 * keys, wide), F32),
            pltpu.VMEM((keys, 4 * keys), F32),
            pltpu.VMEM((keys, 4 * keys), F32),
            pltpu.VMEM((n_i * size, 4 * keys), F32),
        ],
        n_in=6,
    )(*blocks, joined, bias_rows)
    over_core = lax.ppermute(dq_core, "col", flip(1))
    keep, send = call(
        fold_core_kernel,
        "fold_core",
        (struct((quads, keys, LANES), F32), dq_block),
        n_in=3,
    )(dq0, dq2, over_core)
    over_x = lax.ppermute(send, "col", flip(4))
    parts_in = lax.all_to_all(dbias, "row", 0, 0, tiled=True)
    total = call(sum_kernel, "sum", dq_block, n_in=2, cost=SUM_COST)(keep, over_x)
    merged = call(
        merge_kernel,
        "merge",
        (struct((quads + 1, cols, LANES), BF),) * 4,
        n_in=2,
    )(total, parts_in)
    query_grad, kv_grad, bias_grad = call(
        final_kernel,
        "final",
        (
            struct((n_i, cols, width), BF),
            struct((n_i, cols, 2 * width), BF),
            struct((heads, cols, cols), F32),
        ),
        scratch=[
            pltpu.VMEM((heads, quads + 1, cols, LANES), BF),
            pltpu.VMEM((heads, pairs, cols, LANES), BF),
        ],
        n_in=8,
    )(*traded(merged), *traded(dkv))
    kv_grad = jnp.transpose(kv_grad, (1, 0, 2))
    return query_grad, kv_grad, bias_grad


def solution(mesh):
    placed = (
        P("row", "col", None),
        P("row", "col", None),
        P("row", "col", None),
        P(None, "row", "col"),
        P(None, "row", "col"),
        P(None, "row", "col"),
        P(),
    )
    return jax.shard_map(
        on_device,
        mesh=mesh,
        in_specs=placed,
        out_specs=(P("row", "col", None), P("col", "row", None), P(None, "row", "col")),
        check_vma=False,
    )
```

```python
import functools
import math

import jax
import jax.numpy as jnp
from jax import lax
from jax.experimental import pallas as pl
from jax.experimental.pallas import tpu as pltpu
from jax.sharding import PartitionSpec as P

BF = jnp.bfloat16
F32 = jnp.float32
LANES = 128
HEAD_GROUPS = [[0, 2, 12, 14], [1, 3, 13, 15], [4, 6, 8, 10], [5, 7, 9, 11]]


JOIN_COST = pl.CostEstimate(flops=2_000_000_000, bytes_accessed=1_000_000, transcendentals=0)
SUM_COST = pl.CostEstimate(flops=1_000_000_000, bytes_accessed=1_000_000, transcendentals=0)


def flip(bits):
    return [(c, c ^ bits) for c in range(16)]


def trade(step):
    return [(group[p], group[p ^ step]) for group in HEAD_GROUPS for p in range(4)]


def call(body, name, out_shape, scratch=(), n_in=1, space=pltpu.VMEM, limit=48 << 20, cost=None):
    spaces = space if isinstance(space, tuple) else (space,) * n_in
    in_specs = [pl.BlockSpec(memory_space=each) for each in spaces]
    out_specs = jax.tree.map(lambda _: pl.BlockSpec(memory_space=pltpu.VMEM), out_shape)
    return pl.pallas_call(
        body,
        name=name,
        out_shape=out_shape,
        in_specs=in_specs,
        out_specs=out_specs,
        scratch_shapes=list(scratch),
        compiler_params=pltpu.CompilerParams(vmem_limit_bytes=limit),
        cost_estimate=cost,
    )


def place():
    c = lax.axis_index("col")
    x = c // 4
    pair = jnp.bitwise_and(jnp.bitwise_xor(x, x // 2), 1)
    return c, pair, c % 2, (x // 2) * 2 + (c // 2) % 2


def row_of(b, step):
    _, pair, core, position = place()
    there = jnp.bitwise_xor(pair, b // 2)
    to = jnp.bitwise_xor(position, step)
    x = jnp.where(to >= 2, 3 - there, there)
    return x * 4 + (to % 2) * 2 + jnp.bitwise_xor(core, b % 2)


def pack_kernel(root, *refs):
    hbm, out_refs, staged, rows = refs[:7], refs[7:11], refs[11], refs[12]
    local, sems = refs[13:20], refs[20]
    copies = [
        pltpu.make_async_copy(src, dst, sems.at[k])
        for k, (src, dst) in enumerate(zip(hbm, local))
    ]
    for copy in copies:
        copy.start()
    for copy in copies:
        copy.wait()
    q_ref, kv_ref, g_ref, bias_ref, norm_ref, delta_ref, valid_ref = local
    heads, cols, _ = bias_ref.shape
    n_i, _, width = q_ref.shape
    size = width // heads
    pairs = n_i // 2
    count = valid_ref.shape[0]
    valid = jnp.broadcast_to(valid_ref[...].reshape(1, count), (8, count))
    mask = jnp.where(valid == 1, 0.0, -10000.0).astype(F32)
    c, _, _, position = place()
    back = count - c * cols
    mask = pltpu.roll(mask, back, 1)[0:1, 0:cols]
    for h in range(heads):
        lo, hi = h * size, (h + 1) * size
        to = jnp.bitwise_xor(position, h)
        for p in range(pairs):
            staged[to, p] = jnp.concatenate(
                [
                    q_ref[2 * p, :, lo:hi],
                    g_ref[2 * p, :, lo:hi],
                    q_ref[2 * p + 1, :, lo:hi],
                    g_ref[2 * p + 1, :, lo:hi],
                ],
                axis=-1,
            )
            staged[to, pairs + p] = jnp.concatenate(
                [
                    kv_ref[2 * p, :, lo:hi],
                    kv_ref[2 * p, :, width + lo : width + hi],
                    kv_ref[2 * p + 1, :, lo:hi],
                    kv_ref[2 * p + 1, :, width + lo : width + hi],
                ],
                axis=-1,
            )
        rows[...] = jnp.zeros_like(rows)
        norm = norm_ref[:, h, :] * root
        high = norm.astype(BF).astype(F32)
        rows[0:n_i, 0:cols] = high
        rows[16 : 16 + n_i, 0:cols] = norm - high
        delta = delta_ref[:, h, :]
        high = delta.astype(BF).astype(F32)
        rows[32 : 32 + n_i, 0:cols] = high
        rows[48 : 48 + n_i, 0:cols] = delta - high
        turned = jnp.transpose(rows[...])[0:cols]
        tile = bias_ref[h].astype(F32) + mask
        staged[to, 2 * pairs] = jnp.concatenate(
            [turned[:, 0:64], tile, jnp.zeros((cols, 64 - cols), F32)], axis=-1
        ).astype(BF)
    for step in range(heads):
        out_refs[step][...] = staged[step]


def hold_kernel(src_ref, out_ref, sem):
    copy = pltpu.make_async_copy(src_ref, out_ref, sem)
    copy.start()
    copy.wait()


def own_kernel(*refs):
    got, own_ref = refs[0:4], refs[4]
    blocks, cols, _ = got[0].shape
    pairs = blocks // 2
    for step in range(4):
        lo, hi = step * cols, (step + 1) * cols
        own_ref[0:pairs, lo:hi] = got[step][0:pairs]
        own_ref[pairs, lo:hi] = got[step][blocks - 1]


def fold(tile):
    tail = tile[:, LANES : LANES + 64]
    return jnp.concatenate(
        [
            tile[:, 0:LANES],
            jnp.concatenate([tail[0:16], tail[16:32]], axis=1),
            jnp.concatenate([tail[32:48], jnp.zeros((16, 64), tile.dtype)], axis=1),
        ],
        axis=0,
    )


def unfold(tile):
    side = tile[48:64]
    tail = jnp.concatenate([side, pltpu.roll(side, 64, 1), tile[64:80]], axis=0)
    return jnp.concatenate([tile[0:48], tail], axis=1)


def band_kernel(*refs):
    got, bias_ref = refs[0:4], refs[4]
    blocks, cols, _ = got[0].shape
    tiles = [one[blocks - 1, :, 64 : 64 + cols].astype(F32) for one in got]
    band = fold(jnp.concatenate(tiles, axis=-1))
    for r in range(bias_ref.shape[0]):
        bias_ref[r] = band.astype(BF)


def join_kernel(a0_ref, a1_ref, a2_ref, a3_ref, out_ref):
    keys = a0_ref.shape[1]
    for b, a in enumerate((a0_ref, a1_ref, a2_ref, a3_ref)):
        out_ref[:, b * keys : (b + 1) * keys] = a[...]


def main_kernel(inv_root, *refs):
    ab_refs, a_ref, bias_ref = refs[0:4], refs[4], refs[5]
    dq0_ref, dq2_ref, dqc_ref = refs[6:9]
    dkv_refs, dbias_ref = refs[9:13], refs[13]
    rows, bias_t, acc, dq_t = refs[14:]
    blocks, cols, _ = ab_refs[0].shape
    parts = len(ab_refs)
    pairs = blocks // 2
    keys = parts * cols
    total = 4 * keys
    size = 32
    log2e = math.log2(math.e)
    dq_refs = (dq0_ref, dqc_ref.at[0], dq2_ref, dqc_ref.at[1])
    for b in range(4):
        for x in range(parts):
            at = b * keys + x * cols
            rows[at : at + cols] = unfold(bias_ref[row_of(b, x)].astype(F32))
    for t in range(0, total, LANES):
        bias_t[:, t : t + LANES] = (
            jnp.transpose(rows[t : t + LANES])[0:keys] * log2e
        )
    lane = lax.broadcasted_iota(jnp.int32, (keys, LANES), 1)
    quarter = lax.broadcasted_iota(jnp.int32, (total, LANES), 1) // size
    extra = a_ref[pairs]
    scale_row = jnp.where((lane // size) % 2 == 0, inv_root, 1.0)
    def both_of(p):
        qp = a_ref[p]
        qx = jnp.concatenate([qp, extra], axis=1)
        kp = jnp.concatenate([ab[pairs + p] for ab in ab_refs], axis=0)
        kt = jnp.transpose(kp.astype(F32)).astype(BF)
        zero = jnp.zeros_like(kp)
        left = []
        for s in range(4):
            i = 2 * p + s // 2
            base = 32 * (s % 2)
            ones = jnp.where((lane == base + i) | (lane == base + 16 + i), -1.0, 0.0).astype(BF)
            left.append(
                jnp.concatenate([jnp.where(lane // size == s, kp, zero), ones], axis=1)
            )
        return qp, kt, [
            lax.dot_general(
                jnp.concatenate(left[2 * e : 2 * e + 2], axis=0),
                qx,
                (((1,), (1,)), ((), ())),
                preferred_element_type=F32,
            )
            for e in range(2)
        ]

    coming = both_of(0)
    for p in range(pairs):
        qp, kt, both = coming
        if p + 1 < pairs:
            coming = both_of(p + 1)
        low = []
        for e in range(2):
            probs = jnp.exp2(both[e][0:keys] * (inv_root * log2e) + bias_t[...])
            ds = probs * both[e][keys:]
            if p + e == 0:
                acc[...] = ds
            else:
                acc[...] += ds
            low += [ds.astype(BF), probs.astype(BF)]
            i = 2 * p + e
            dq_t[i * size : (i + 1) * size] = jnp.dot(
                kt[2 * e * size : (2 * e + 1) * size], low[2 * e], preferred_element_type=F32
            )
        out = jnp.zeros((keys, LANES), F32)
        for s in range(4):
            out += jnp.dot(
                low[s], jnp.where(quarter == s, qp, jnp.zeros_like(qp)), preferred_element_type=F32
            )
        out = (out * scale_row).astype(BF)
        for step in range(parts):
            dkv_refs[step][p] = out[step * cols : (step + 1) * cols]
    for quad in range(2 * pairs // 4):
        turned = jnp.transpose(dq_t[quad * LANES : (quad + 1) * LANES]) * inv_root
        for b in range(4):
            dq_refs[b][quad] = turned[b * keys : (b + 1) * keys].astype(BF)
    for t in range(0, total, LANES):
        rows[t : t + LANES, 0:keys] = jnp.transpose(acc[:, t : t + LANES])
    for b in range(4):
        for x in range(parts):
            at = b * keys + x * cols
            dbias_ref[row_of(b, x)] = fold(rows[at : at + cols]).astype(BF)


def fold_core_kernel(dq0_ref, dq2_ref, got_ref, keep_ref, send_ref):
    keep_ref[...] = dq0_ref[...].astype(F32) + got_ref[0].astype(F32)
    send_ref[...] = (dq2_ref[...].astype(F32) + got_ref[1].astype(F32)).astype(BF)


def sum_kernel(keep_ref, got_ref, out_ref):
    out_ref[...] = (keep_ref[...] + got_ref[...].astype(F32)).astype(BF)


def merge_kernel(total, db_ref, *out_refs):
    quads = total.shape[0]
    cols = out_refs[0].shape[1]
    bias = db_ref[0].astype(F32)
    for r in range(1, db_ref.shape[0]):
        bias = bias + db_ref[r].astype(F32)
    bias = unfold(bias)
    for step, out_ref in enumerate(out_refs):
        lo, hi = step * cols, (step + 1) * cols
        out_ref[0:quads] = total[:, lo:hi]
        out_ref[quads] = jnp.concatenate(
            [bias[:, lo:hi], jnp.zeros((cols, LANES - cols), F32)], axis=-1
        ).astype(BF)


def final_kernel(*refs):
    f_refs, kv_refs = refs[0:4], refs[4:8]
    dq_ref, dkv_ref, db_ref, f_all, kv_all = refs[8:]
    heads, cols = len(f_refs), dq_ref.shape[1]
    size = 32
    n_i = dq_ref.shape[0]
    quads = n_i // 4
    position = place()[3]
    for step in range(heads):
        h = jnp.bitwise_xor(position, step)
        f_all[h] = f_refs[step][...]
        kv_all[h] = kv_refs[step][...]
    for i in range(n_i):
        at = (i % 4) * size
        dq_ref[i] = jnp.concatenate(
            [f_all[h, i // 4, :, at : at + size] for h in range(heads)], axis=-1
        )
        at = (i % 2) * 2 * size
        dkv_ref[i] = jnp.concatenate(
            [kv_all[h, i // 2, :, at : at + size] for h in range(heads)]
            + [kv_all[h, i // 2, :, at + size : at + 2 * size] for h in range(heads)],
            axis=-1,
        )
    for h in range(heads):
        db_ref[h] = f_all[h, quads, :, 0:cols].astype(F32)


def on_device(queries, keys_values, out_grad, pair_bias, log_norm, delta_rows, token_valid):
    n_i, cols, width = queries.shape
    heads = pair_bias.shape[0]
    size = width // heads
    pairs = n_i // 2
    quads = n_i // 4
    n_rows = lax.axis_size("row")
    keys = heads * cols
    wide = 2 * LANES
    struct = jax.ShapeDtypeStruct
    inputs = (
        queries,
        keys_values,
        out_grad,
        pair_bias,
        jnp.transpose(log_norm, (1, 0, 2)),
        jnp.transpose(delta_rows, (1, 0, 2)),
        token_valid,
    )

    def traded(blocks):
        return [blocks[0]] + [lax.ppermute(blocks[k], "col", trade(k)) for k in (1, 2, 3)]

    sent = call(
        functools.partial(pack_kernel, math.sqrt(size)),
        "pack",
        (struct((2 * pairs + 1, cols, LANES), BF),) * 4,
        scratch=[
            pltpu.VMEM((heads, 2 * pairs + 1, cols, LANES), BF),
            pltpu.VMEM((64, LANES), F32),
        ]
        + [pltpu.VMEM(v.shape, v.dtype) for v in inputs]
        + [pltpu.SemaphoreType.DMA((len(inputs),))],
        n_in=len(inputs),
        space=pltpu.HBM,
        limit=62 << 20,
    )(*inputs)
    held = call(
        hold_kernel,
        "hold",
        struct(sent[0].shape, BF),
        scratch=[pltpu.SemaphoreType.DMA],
        space=pltpu.HBM,
    )(sent[0])
    blocks = [held] + traded(sent)[1:]
    own = call(own_kernel, "own", struct((pairs + 1, keys, LANES), BF), n_in=4)(*blocks)
    over_x = lax.ppermute(own, "col", flip(4))
    over_core = lax.ppermute(own, "col", flip(1))
    folded = struct((n_rows, 80, LANES), BF)
    dq_block = struct((quads, keys, LANES), BF)
    band = call(band_kernel, "band", folded, n_in=4)(*blocks)
    bias_rows = lax.all_to_all(band, "row", 0, 0, tiled=True)
    over_both = lax.ppermute(over_x, "col", flip(1))
    joined = call(
        join_kernel,
        "join",
        struct((pairs + 1, 4 * keys, LANES), BF),
        n_in=4,
        cost=JOIN_COST,
    )(own, over_core, over_x, over_both)
    dq0, dq2, dq_core, *dkv, dbias = call(
        functools.partial(main_kernel, size**-0.5),
        "main",
        (
            dq_block,
            dq_block,
            struct((2, quads, keys, LANES), BF),
        )
        + (struct((pairs, cols, LANES), BF),) * 4
        + (folded,),
        scratch=[
            pltpu.VMEM((4 * keys, wide), F32),
            pltpu.VMEM((keys, 4 * keys), F32),
            pltpu.VMEM((keys, 4 * keys), F32),
            pltpu.VMEM((n_i * size, 4 * keys), F32),
        ],
        n_in=6,
    )(*blocks, joined, bias_rows)
    over_core = lax.ppermute(dq_core, "col", flip(1))
    keep, send = call(
        fold_core_kernel,
        "fold_core",
        (struct((quads, keys, LANES), F32), dq_block),
        n_in=3,
    )(dq0, dq2, over_core)
    over_x = lax.ppermute(send, "col", flip(4))
    parts_in = lax.all_to_all(dbias, "row", 0, 0, tiled=True)
    total = call(sum_kernel, "sum", dq_block, n_in=2, cost=SUM_COST)(keep, over_x)
    merged = call(
        merge_kernel,
        "merge",
        (struct((quads + 1, cols, LANES), BF),) * 4,
        n_in=2,
    )(total, parts_in)
    query_grad, kv_grad, bias_grad = call(
        final_kernel,
        "final",
        (
            struct((n_i, cols, width), BF),
            struct((n_i, cols, 2 * width), BF),
            struct((heads, cols, cols), F32),
        ),
        scratch=[
            pltpu.VMEM((heads, quads + 1, cols, LANES), BF),
            pltpu.VMEM((heads, pairs, cols, LANES), BF),
        ],
        n_in=8,
    )(*traded(merged), *traded(dkv))
    kv_grad = jnp.transpose(kv_grad, (1, 0, 2))
    return query_grad, kv_grad, bias_grad


def solution(mesh):
    placed = (
        P("row", "col", None),
        P("row", "col", None),
        P("row", "col", None),
        P(None, "row", "col"),
        P(None, "row", "col"),
        P(None, "row", "col"),
        P(),
    )
    return jax.shard_map(
        on_device,
        mesh=mesh,
        in_specs=placed,
        out_specs=(P("row", "col", None), P("col", "row", None), P(None, "row", "col")),
        check_vma=False,
    )
```

```python
import functools
import math

import jax
import jax.numpy as jnp
from jax import lax
from jax.experimental import pallas as pl
from jax.experimental.pallas import tpu as pltpu
from jax.sharding import PartitionSpec as P

BF = jnp.bfloat16
F32 = jnp.float32
LANES = 128
HEAD_GROUPS = [[0, 2, 12, 14], [1, 3, 13, 15], [4, 6, 8, 10], [5, 7, 9, 11]]


JOIN_COST = pl.CostEstimate(flops=2_000_000_000, bytes_accessed=1_000_000, transcendentals=0)
SUM_COST = pl.CostEstimate(flops=1_000_000_000, bytes_accessed=1_000_000, transcendentals=0)


def flip(bits):
    return [(c, c ^ bits) for c in range(16)]


def trade(step):
    return [(group[p], group[p ^ step]) for group in HEAD_GROUPS for p in range(4)]


def call(body, name, out_shape, scratch=(), n_in=1, space=pltpu.VMEM, limit=48 << 20, cost=None):
    spaces = space if isinstance(space, tuple) else (space,) * n_in
    in_specs = [pl.BlockSpec(memory_space=each) for each in spaces]
    out_specs = jax.tree.map(lambda _: pl.BlockSpec(memory_space=pltpu.VMEM), out_shape)
    return pl.pallas_call(
        body,
        name=name,
        out_shape=out_shape,
        in_specs=in_specs,
        out_specs=out_specs,
        scratch_shapes=list(scratch),
        compiler_params=pltpu.CompilerParams(vmem_limit_bytes=limit),
        cost_estimate=cost,
    )


def place():
    c = lax.axis_index("col")
    x = c // 4
    pair = jnp.bitwise_and(jnp.bitwise_xor(x, x // 2), 1)
    return c, pair, c % 2, (x // 2) * 2 + (c // 2) % 2


def row_of(b, step):
    _, pair, core, position = place()
    there = jnp.bitwise_xor(pair, b // 2)
    to = jnp.bitwise_xor(position, step)
    x = jnp.where(to >= 2, 3 - there, there)
    return x * 4 + (to % 2) * 2 + jnp.bitwise_xor(core, b % 2)


def pack_kernel(root, *refs):
    hbm, out_refs, staged, rows = refs[:7], refs[7:11], refs[11], refs[12]
    local, sems = refs[13:20], refs[20]
    copies = [
        pltpu.make_async_copy(src, dst, sems.at[k])
        for k, (src, dst) in enumerate(zip(hbm, local))
    ]
    for copy in copies:
        copy.start()
    for k in (3, 4, 5, 6):
        copies[k].wait()
    q_ref, kv_ref, g_ref, bias_ref, norm_ref, delta_ref, valid_ref = local
    heads, cols, _ = bias_ref.shape
    n_i, _, width = q_ref.shape
    size = width // heads
    pairs = n_i // 2
    count = valid_ref.shape[0]
    valid = jnp.broadcast_to(valid_ref[...].reshape(1, count), (8, count))
    mask = jnp.where(valid == 1, 0.0, -10000.0).astype(F32)
    c, _, _, position = place()
    back = count - c * cols
    mask = pltpu.roll(mask, back, 1)[0:1, 0:cols]
    for h in range(heads):
        to = jnp.bitwise_xor(position, h)
        rows[...] = jnp.zeros_like(rows)
        norm = norm_ref[:, h, :] * root
        high = norm.astype(BF).astype(F32)
        rows[0:n_i, 0:cols] = high
        rows[16 : 16 + n_i, 0:cols] = norm - high
        delta = delta_ref[:, h, :]
        high = delta.astype(BF).astype(F32)
        rows[32 : 32 + n_i, 0:cols] = high
        rows[48 : 48 + n_i, 0:cols] = delta - high
        turned = jnp.transpose(rows[...])[0:cols]
        tile = bias_ref[h].astype(F32) + mask
        staged[to, 2 * pairs] = jnp.concatenate(
            [turned[:, 0:64], tile, jnp.zeros((cols, 64 - cols), F32)], axis=-1
        ).astype(BF)
    copies[0].wait()
    copies[2].wait()
    for h in range(heads):
        lo, hi = h * size, (h + 1) * size
        to = jnp.bitwise_xor(position, h)
        for p in range(pairs):
            staged[to, p] = jnp.concatenate(
                [
                    q_ref[2 * p, :, lo:hi],
                    g_ref[2 * p, :, lo:hi],
                    q_ref[2 * p + 1, :, lo:hi],
                    g_ref[2 * p + 1, :, lo:hi],
                ],
                axis=-1,
            )
    copies[1].wait()
    for h in range(heads):
        lo, hi = h * size, (h + 1) * size
        to = jnp.bitwise_xor(position, h)
        for p in range(pairs):
            staged[to, pairs + p] = jnp.concatenate(
                [
                    kv_ref[2 * p, :, lo:hi],
                    kv_ref[2 * p, :, width + lo : width + hi],
                    kv_ref[2 * p + 1, :, lo:hi],
                    kv_ref[2 * p + 1, :, width + lo : width + hi],
                ],
                axis=-1,
            )
    for step in range(heads):
        out_refs[step][...] = staged[step]


def hold_kernel(src_ref, out_ref, sem):
    copy = pltpu.make_async_copy(src_ref, out_ref, sem)
    copy.start()
    copy.wait()


def own_kernel(*refs):
    got, own_ref = refs[0:4], refs[4]
    blocks, cols, _ = got[0].shape
    pairs = blocks // 2
    for step in range(4):
        lo, hi = step * cols, (step + 1) * cols
        own_ref[0:pairs, lo:hi] = got[step][0:pairs]
        own_ref[pairs, lo:hi] = got[step][blocks - 1]


def fold(tile):
    tail = tile[:, LANES : LANES + 64]
    return jnp.concatenate(
        [
            tile[:, 0:LANES],
            jnp.concatenate([tail[0:16], tail[16:32]], axis=1),
            jnp.concatenate([tail[32:48], jnp.zeros((16, 64), tile.dtype)], axis=1),
        ],
        axis=0,
    )


def unfold(tile):
    side = tile[48:64]
    tail = jnp.concatenate([side, pltpu.roll(side, 64, 1), tile[64:80]], axis=0)
    return jnp.concatenate([tile[0:48], tail], axis=1)


def band_kernel(*refs):
    got, bias_ref = refs[0:4], refs[4]
    blocks, cols, _ = got[0].shape
    tiles = [one[blocks - 1, :, 64 : 64 + cols].astype(F32) for one in got]
    band = fold(jnp.concatenate(tiles, axis=-1))
    for r in range(bias_ref.shape[0]):
        bias_ref[r] = band.astype(BF)


def join_kernel(a0_ref, a1_ref, a2_ref, a3_ref, out_ref):
    keys = a0_ref.shape[1]
    for b, a in enumerate((a0_ref, a1_ref, a2_ref, a3_ref)):
        out_ref[:, b * keys : (b + 1) * keys] = a[...]


def main_kernel(inv_root, *refs):
    ab_refs, a_ref, bias_ref = refs[0:4], refs[4], refs[5]
    dq0_ref, dq2_ref, dqc_ref = refs[6:9]
    dkv_refs, dbias_ref = refs[9:13], refs[13]
    rows, bias_t, acc, dq_t = refs[14:]
    blocks, cols, _ = ab_refs[0].shape
    parts = len(ab_refs)
    pairs = blocks // 2
    keys = parts * cols
    total = 4 * keys
    size = 32
    log2e = math.log2(math.e)
    dq_refs = (dq0_ref, dqc_ref.at[0], dq2_ref, dqc_ref.at[1])
    for b in range(4):
        for x in range(parts):
            at = b * keys + x * cols
            rows[at : at + cols] = unfold(bias_ref[row_of(b, x)].astype(F32))
    for t in range(0, total, LANES):
        bias_t[:, t : t + LANES] = (
            jnp.transpose(rows[t : t + LANES])[0:keys] * log2e
        )
    lane = lax.broadcasted_iota(jnp.int32, (keys, LANES), 1)
    quarter = lax.broadcasted_iota(jnp.int32, (total, LANES), 1) // size
    extra = a_ref[pairs]
    scale_row = jnp.where((lane // size) % 2 == 0, inv_root, 1.0)
    def both_of(p):
        qp = a_ref[p]
        qx = jnp.concatenate([qp, extra], axis=1)
        kp = jnp.concatenate([ab[pairs + p] for ab in ab_refs], axis=0)
        kt = jnp.transpose(kp.astype(F32)).astype(BF)
        zero = jnp.zeros_like(kp)
        left = []
        for s in range(4):
            i = 2 * p + s // 2
            base = 32 * (s % 2)
            ones = jnp.where((lane == base + i) | (lane == base + 16 + i), -1.0, 0.0).astype(BF)
            left.append(
                jnp.concatenate([jnp.where(lane // size == s, kp, zero), ones], axis=1)
            )
        return qp, kt, [
            lax.dot_general(
                jnp.concatenate(left[2 * e : 2 * e + 2], axis=0),
                qx,
                (((1,), (1,)), ((), ())),
                preferred_element_type=F32,
            )
            for e in range(2)
        ]

    coming = both_of(0)
    for p in range(pairs):
        qp, kt, both = coming
        if p + 1 < pairs:
            coming = both_of(p + 1)
        low = []
        for e in range(2):
            probs = jnp.exp2(both[e][0:keys] * (inv_root * log2e) + bias_t[...])
            ds = probs * both[e][keys:]
            if p + e == 0:
                acc[...] = ds
            else:
                acc[...] += ds
            low += [ds.astype(BF), probs.astype(BF)]
            i = 2 * p + e
            dq_t[i * size : (i + 1) * size] = jnp.dot(
                kt[2 * e * size : (2 * e + 1) * size], low[2 * e], preferred_element_type=F32
            )
        out = jnp.zeros((keys, LANES), F32)
        for s in range(4):
            out += jnp.dot(
                low[s], jnp.where(quarter == s, qp, jnp.zeros_like(qp)), preferred_element_type=F32
            )
        out = (out * scale_row).astype(BF)
        for step in range(parts):
            dkv_refs[step][p] = out[step * cols : (step + 1) * cols]
    for quad in range(2 * pairs // 4):
        turned = jnp.transpose(dq_t[quad * LANES : (quad + 1) * LANES]) * inv_root
        for b in range(4):
            dq_refs[b][quad] = turned[b * keys : (b + 1) * keys].astype(BF)
    for t in range(0, total, LANES):
        rows[t : t + LANES, 0:keys] = jnp.transpose(acc[:, t : t + LANES])
    for b in range(4):
        for x in range(parts):
            at = b * keys + x * cols
            dbias_ref[row_of(b, x)] = fold(rows[at : at + cols]).astype(BF)


def fold_core_kernel(dq0_ref, dq2_ref, got_ref, keep_ref, send_ref):
    keep_ref[...] = dq0_ref[...].astype(F32) + got_ref[0].astype(F32)
    send_ref[...] = (dq2_ref[...].astype(F32) + got_ref[1].astype(F32)).astype(BF)


def sum_kernel(keep_ref, got_ref, out_ref):
    out_ref[...] = (keep_ref[...] + got_ref[...].astype(F32)).astype(BF)


def merge_kernel(total, db_ref, *out_refs):
    quads = total.shape[0]
    cols = out_refs[0].shape[1]
    bias = db_ref[0].astype(F32)
    for r in range(1, db_ref.shape[0]):
        bias = bias + db_ref[r].astype(F32)
    bias = unfold(bias)
    for step, out_ref in enumerate(out_refs):
        lo, hi = step * cols, (step + 1) * cols
        out_ref[0:quads] = total[:, lo:hi]
        out_ref[quads] = jnp.concatenate(
            [bias[:, lo:hi], jnp.zeros((cols, LANES - cols), F32)], axis=-1
        ).astype(BF)


def final_kernel(*refs):
    f_refs, kv_refs = refs[0:4], refs[4:8]
    dq_ref, dkv_ref, db_ref, f_all, kv_all = refs[8:]
    heads, cols = len(f_refs), dq_ref.shape[1]
    size = 32
    n_i = dq_ref.shape[0]
    quads = n_i // 4
    position = place()[3]
    for step in range(heads):
        h = jnp.bitwise_xor(position, step)
        f_all[h] = f_refs[step][...]
        kv_all[h] = kv_refs[step][...]
    for i in range(n_i):
        at = (i % 4) * size
        dq_ref[i] = jnp.concatenate(
            [f_all[h, i // 4, :, at : at + size] for h in range(heads)], axis=-1
        )
        at = (i % 2) * 2 * size
        dkv_ref[i] = jnp.concatenate(
            [kv_all[h, i // 2, :, at : at + size] for h in range(heads)]
            + [kv_all[h, i // 2, :, at + size : at + 2 * size] for h in range(heads)],
            axis=-1,
        )
    for h in range(heads):
        db_ref[h] = f_all[h, quads, :, 0:cols].astype(F32)


def on_device(queries, keys_values, out_grad, pair_bias, log_norm, delta_rows, token_valid):
    n_i, cols, width = queries.shape
    heads = pair_bias.shape[0]
    size = width // heads
    pairs = n_i // 2
    quads = n_i // 4
    n_rows = lax.axis_size("row")
    keys = heads * cols
    wide = 2 * LANES
    struct = jax.ShapeDtypeStruct
    inputs = (
        queries,
        keys_values,
        out_grad,
        pair_bias,
        jnp.transpose(log_norm, (1, 0, 2)),
        jnp.transpose(delta_rows, (1, 0, 2)),
        token_valid,
    )

    def traded(blocks):
        return [blocks[0]] + [lax.ppermute(blocks[k], "col", trade(k)) for k in (1, 2, 3)]

    sent = call(
        functools.partial(pack_kernel, math.sqrt(size)),
        "pack",
        (struct((2 * pairs + 1, cols, LANES), BF),) * 4,
        scratch=[
            pltpu.VMEM((heads, 2 * pairs + 1, cols, LANES), BF),
            pltpu.VMEM((64, LANES), F32),
        ]
        + [pltpu.VMEM(v.shape, v.dtype) for v in inputs]
        + [pltpu.SemaphoreType.DMA((len(inputs),))],
        n_in=len(inputs),
        space=pltpu.HBM,
        limit=62 << 20,
    )(*inputs)
    held = call(
        hold_kernel,
        "hold",
        struct(sent[0].shape, BF),
        scratch=[pltpu.SemaphoreType.DMA],
        space=pltpu.HBM,
    )(sent[0])
    blocks = [held] + traded(sent)[1:]
    own = call(own_kernel, "own", struct((pairs + 1, keys, LANES), BF), n_in=4)(*blocks)
    over_x = lax.ppermute(own, "col", flip(4))
    over_core = lax.ppermute(own, "col", flip(1))
    folded = struct((n_rows, 80, LANES), BF)
    dq_block = struct((quads, keys, LANES), BF)
    band = call(band_kernel, "band", folded, n_in=4)(*blocks)
    bias_rows = lax.all_to_all(band, "row", 0, 0, tiled=True)
    over_both = lax.ppermute(over_x, "col", flip(1))
    joined = call(
        join_kernel,
        "join",
        struct((pairs + 1, 4 * keys, LANES), BF),
        n_in=4,
        cost=JOIN_COST,
    )(own, over_core, over_x, over_both)
    dq0, dq2, dq_core, *dkv, dbias = call(
        functools.partial(main_kernel, size**-0.5),
        "main",
        (
            dq_block,
            dq_block,
            struct((2, quads, keys, LANES), BF),
        )
        + (struct((pairs, cols, LANES), BF),) * 4
        + (folded,),
        scratch=[
            pltpu.VMEM((4 * keys, wide), F32),
            pltpu.VMEM((keys, 4 * keys), F32),
            pltpu.VMEM((keys, 4 * keys), F32),
            pltpu.VMEM((n_i * size, 4 * keys), F32),
        ],
        n_in=6,
    )(*blocks, joined, bias_rows)
    over_core = lax.ppermute(dq_core, "col", flip(1))
    keep, send = call(
        fold_core_kernel,
        "fold_core",
        (struct((quads, keys, LANES), F32), dq_block),
        n_in=3,
    )(dq0, dq2, over_core)
    over_x = lax.ppermute(send, "col", flip(4))
    parts_in = lax.all_to_all(dbias, "row", 0, 0, tiled=True)
    total = call(sum_kernel, "sum", dq_block, n_in=2, cost=SUM_COST)(keep, over_x)
    merged = call(
        merge_kernel,
        "merge",
        (struct((quads + 1, cols, LANES), BF),) * 4,
        n_in=2,
    )(total, parts_in)
    query_grad, kv_grad, bias_grad = call(
        final_kernel,
        "final",
        (
            struct((n_i, cols, width), BF),
            struct((n_i, cols, 2 * width), BF),
            struct((heads, cols, cols), F32),
        ),
        scratch=[
            pltpu.VMEM((heads, quads + 1, cols, LANES), BF),
            pltpu.VMEM((heads, pairs, cols, LANES), BF),
        ],
        n_in=8,
    )(*traded(merged), *traded(dkv))
    kv_grad = jnp.transpose(kv_grad, (1, 0, 2))
    return query_grad, kv_grad, bias_grad


def solution(mesh):
    placed = (
        P("row", "col", None),
        P("row", "col", None),
        P("row", "col", None),
        P(None, "row", "col"),
        P(None, "row", "col"),
        P(None, "row", "col"),
        P(),
    )
    return jax.shard_map(
        on_device,
        mesh=mesh,
        in_specs=placed,
        out_specs=(P("row", "col", None), P("col", "row", None), P(None, "row", "col")),
        check_vma=False,
    )
```
